256 devices in a mesh: var: 8 (over x, z_hi), seq: 32 (over z_lo, y, core).
Axes of the slice: x: 4, y: 4, z: 8 (z_hi: 2, z_lo: 4; z = z_hi * 4 + z_lo), core: 2. Of those that a mesh axis runs over, the one named last changes fastest.
Arguments:
- patches: bfloat16 [96, 16, 8192], P(None, None, 'seq'), may hold values from -6 to 6
- embed_weight: bfloat16 [96, 16, 4096], P(None, None, 'var'), may hold values from -1.5 to 1.5
- var_embed: bfloat16 [96, 4096], P(None, 'var'), may hold values from -3 to 3
- key_query: bfloat16 [4096, 32], P('var'), may hold values from -0.1875 to 0.1875
- var_mask: int32 [96], replicated, may hold values from 0 to 1, as said below
- value_weight: bfloat16 [4096, 32, 128], P('var', 'seq'), may hold values from -0.1875 to 0.1875
- out_weight: bfloat16 [4096, 4096], P('var', 'seq'), may hold values from -0.1875 to 0.1875
- out_bias: bfloat16 [4096], P('var'), may hold values from -3 to 3
Outputs:
- aggregated_tokens: bfloat16 [8192, 4096], P('seq', 'var')
The draws below stay inside these ranges and needn't reach their ends.
Inputs may be any that keep to these rules, and one draw needn't show every extreme that they name: `var_mask`: exactly 91 entries are 1.
All inputs are finite; a program needn't handle non-finite values.
Results may differ from the reference program's by a relative error of at most 0.025.
Values may be sent and summed in bfloat16 or wider, within the bound.
A program may use at most 128 MiB of HBM per device.

```python
import jax
import jax.numpy as jnp
from jax import lax

D = 4096
HEADS = 32
HEAD_DIM = 128
VARS = 96
REAL_VARS = 91
PIX = 16
TOK_DEV = 256
TOKENS = 8192


def draw_var_mask(key, part):
    key = jax.random.fold_in(key, 7)
    order = jax.random.permutation(key, VARS)
    return jnp.where(order < REAL_VARS, 1, 0).astype(jnp.int32)


def with_spikes(array, rng, source, target, blocks, factor):
    owner, partner = [(jnp.arange(array.shape[position]) // (array.shape[position] // blocks)).reshape([-1 if axis == position else 1 for axis in range(array.ndim)]) for position in (source, target)]
    chosen = jax.random.permutation(rng, blocks)[partner]
    strong = (owner == chosen) | (owner == (partner + blocks // 2) % blocks)
    return jnp.where(strong, factor * array, array)


def level_of(stream_key, dims, cuts, smallest, largest):
    def one(dim, parts):
        draws = jax.random.uniform(jax.random.fold_in(jax.random.fold_in(stream_key, 6), dim), (parts,), jnp.float32, smallest / len(cuts), largest / len(cuts))
        return jnp.repeat(jnp.exp(draws), dims[dim] // parts).reshape((-1,) + (1,) * (len(dims) - dim - 1))

    gain = one(*cuts[0])
    for cut in cuts[1:]:
        gain = gain * one(*cut)
    return gain


def scatter_about(rng, extent, scale, reach, shards=(), dtype=jnp.bfloat16):
    gain = level_of(rng, extent, shards, -0.22, 0.18) if shards else 1.0
    values = jax.random.normal(rng, extent, jnp.float32) * scale * gain
    return jnp.minimum(jnp.maximum(values, -reach), reach).astype(dtype)


def bell_draw_with(stream_key, extent, scale, most, pieces, heavy, kind=jnp.bfloat16):
    array = scale * jax.random.normal(stream_key, extent, jnp.float32)
    if pieces:
        array = array * level_of(stream_key, extent, pieces, -0.22, 0.18)
    return jnp.clip(with_spikes(array, jax.random.fold_in(stream_key, 3), *heavy), -most, most).astype(kind)


def setup_inputs(seed: int = 0) -> dict:
    key_of = jax.random.split(jax.random.key(seed), 9)
    return {
        "patches": scatter_about(key_of[0], (VARS, PIX, TOKENS), 1.0, 6.0, ((2, 32),)),
        "embed_weight": scatter_about(key_of[1], (VARS, PIX, D), PIX ** -0.5, 1.5, ((2, 8),)),
        "var_embed": scatter_about(key_of[2], (VARS, D), 0.5, 3.0, ((1, 8),)),
        "key_query": scatter_about(key_of[3], (D, HEADS), (D // 4) ** -0.5, 0.1875, ((0, 8),)),
        "var_mask": draw_var_mask(jax.random.fold_in(key_of[8], 71), 0),
        "value_weight": bell_draw_with(key_of[5], (D, HEADS, HEAD_DIM), D ** -0.5, 0.1875, ((0, 8), (1, 32)), (0, 1, 32, 2.75)),
        "out_weight": bell_draw_with(key_of[6], (D, D), D ** -0.5, 0.1875, ((0, 8), (1, 32)), (0, 1, 32, 2.75)),
        "out_bias": scatter_about(key_of[7], (D,), 0.5, 3.0, ((0, 8),)),
    }


def reference(patches, embed_weight, var_embed, key_query, var_mask, value_weight, out_weight, out_bias):
    width = TOK_DEV
    count = TOKENS // width
    blocks = jnp.moveaxis(patches.reshape(VARS, PIX, count, width), 2, 0)
    maskf = var_mask.astype(jnp.float32)[None, :, None]

    def one_block(piece):
        embedded = jnp.einsum('vpt,vpd->vtd', piece.astype(jnp.float32), embed_weight.astype(jnp.float32))
        embedded = (embedded + var_embed.astype(jnp.float32)[:, None, :]).astype(jnp.bfloat16)
        scores = jnp.einsum('vtd,dh->hvt', embedded.astype(jnp.float32), key_query.astype(jnp.float32))
        raised = jnp.exp(scores) * maskf
        attention = (raised / jnp.sum(raised, axis=1, keepdims=True)).astype(jnp.bfloat16)
        pooled = jnp.einsum('hvt,vtd->htd', attention.astype(jnp.float32), embedded.astype(jnp.float32)).astype(jnp.bfloat16)
        projected = jnp.einsum('htd,dhe->the', pooled.astype(jnp.float32), value_weight.astype(jnp.float32))
        projected = projected.astype(jnp.bfloat16).reshape(width, D)
        result = jnp.dot(projected, out_weight, preferred_element_type=jnp.float32) + out_bias.astype(jnp.float32)
        return result.astype(jnp.bfloat16)

    return lax.map(one_block, blocks).reshape(TOKENS, D)
```

```python
import jax
import jax.numpy as jnp
from jax import lax
from jax.sharding import PartitionSpec as P


def normalize(scores, var_mask):
    raised = jnp.exp(scores) * var_mask.astype(jnp.float32)[None, :, None]
    return (raised / jnp.sum(raised, axis=1, keepdims=True)).astype(jnp.bfloat16)


def local(
    patches, embed_weight, var_embed, key_query, var_mask, value_weight, out_weight, out_bias
):
    folded_query = lax.psum(
        jnp.concatenate(
            [
                jnp.einsum(
                    "vpd,dh->vph", embed_weight, key_query, preferred_element_type=jnp.float32
                ),
                jnp.dot(var_embed, key_query, preferred_element_type=jnp.float32)[:, None, :],
            ],
            axis=1,
        ),
        "var",
    )
    scores = (
        jnp.einsum(
            "vph,vpt->hvt",
            folded_query[:, :16],
            patches.astype(jnp.float32),
            precision=lax.Precision.HIGHEST,
        )
        + folded_query[:, 16].T[:, :, None]
    )
    attention = normalize(scores, var_mask)
    embedded = jnp.einsum("vpt,vpd->vtd", patches, embed_weight, preferred_element_type=jnp.float32)
    embedded = (embedded + var_embed.astype(jnp.float32)[:, None, :]).astype(jnp.bfloat16)
    pooled = jnp.einsum(
        "hvt,vtd->htd", attention, embedded, preferred_element_type=jnp.float32
    ).astype(jnp.bfloat16)
    tok_rows = pooled.shape[1]
    partial_heads = jnp.einsum(
        "htd,dhe->the",
        pooled,
        lax.all_gather(value_weight, "seq", axis=1, tiled=True),
        preferred_element_type=jnp.float32,
    )
    partial_values = partial_heads.reshape(tok_rows, -1)
    projected = lax.psum_scatter(
        partial_values.astype(jnp.bfloat16), "var", scatter_dimension=1, tiled=True
    )
    partial_out = jnp.dot(
        projected,
        lax.all_gather(out_weight, "seq", axis=1, tiled=True),
        preferred_element_type=jnp.float32,
    )
    summed = lax.psum_scatter(
        partial_out.astype(jnp.bfloat16), "var", scatter_dimension=1, tiled=True
    ).astype(jnp.float32)
    return (summed + out_bias.astype(jnp.float32)[None, :]).astype(jnp.bfloat16)


def solution(mesh):
    placed = (
        P(None, None, "seq"),
        P(None, None, "var"),
        P(None, "var"),
        P("var", None),
        P(),
        P("var", "seq", None),
        P("var", "seq"),
        P("var"),
    )
    return jax.shard_map(
        local, mesh=mesh, in_specs=placed, out_specs=P("seq", "var"), check_vma=False
    )
```

```python
import jax
import jax.numpy as jnp
from jax import lax
from jax.experimental import pallas as pl
from jax.experimental.pallas import tpu as pltpu
from jax.sharding import PartitionSpec as P

MESH = pl.DeviceIdType.MESH
F32 = jnp.float32
BF16 = jnp.bfloat16
VARS, PIX, TOK = 96, 16, 256
ROWS = VARS * PIX
DEPTH = ROWS + 128
CHUNK = 256
VAR_CHUNK = CHUNK // PIX
HEADS_DEV = 4
COLS = 512


def iota(shape, dim):
    return lax.broadcasted_iota(jnp.int32, shape, dim)


def kernel(
    patches,
    weight,
    embed,
    left_side,
    mask,
    out_weight,
    bias,
    out,
    o_all,
    u_all,
    table_out,
    table_in,
    u_part,
    u_in_x,
    u_mid,
    u_in_z,
    embed_pad,
    table,
    scores,
    attention,
    weighted,
    heads,
    total,
    o_send,
    o_recv,
    u_send,
    u_recv,
    o_swap,
    t_send,
    t_recv,
    x_send,
    x_recv,
    z_send,
    z_recv,
    p_send,
    p_recv,
):
    me = lax.axis_index("var")
    seat = lax.axis_index("seq")
    x, half = lax.div(me, 2), lax.rem(me, 2)
    zlo, y, core = lax.div(seat, 8), lax.rem(lax.div(seat, 2), 4), lax.rem(seat, 2)

    def place(dz, dy, dc=0):
        return (
            lax.rem(zlo + dz + 4, 4) * 8 + lax.rem(y + dy + 4, 4) * 2 + lax.rem(core + dc, 2)
        )

    def remote(src, dst, send, recv, device):
        return pltpu.make_async_remote_copy(
            src_ref=src,
            dst_ref=dst,
            send_sem=send,
            recv_sem=recv,
            device_id=device,
            device_id_type=MESH,
        )

    sent = []

    def go(*args):
        copy = remote(*args)
        copy.start()
        sent.append(copy)

    class Gather:
        def __init__(self, buf, send, recv):
            self.buf, self.send, self.recv, self.count = buf, send, recv, 0

        def push(self, piece, target):
            go(
                self.buf.at[piece],
                self.buf.at[piece],
                self.send.at[self.count],
                self.recv.at[piece],
                (me, target),
            )
            self.count += 1

        def arrive(self, piece):
            remote(
                self.buf.at[piece],
                self.buf.at[piece],
                self.send.at[0],
                self.recv.at[piece],
                (me, seat),
            ).wait_recv()

        def own(self):
            for dz in (1, 2, 3):
                self.push(seat, place(dz, 0))
            self.sides(seat)

        def sides(self, piece):
            self.push(piece, place(0, 1))
            self.push(piece, place(0, -1))
            self.push(piece, place(0, 0, 1))

        def line(self):
            for dz in (1, 2, 3):
                piece = place(-dz, 0)
                self.arrive(piece)
                self.sides(piece)

        def ring(self):
            for dz in range(4):
                left, right = place(-dz, -1), place(-dz, 1)
                self.arrive(left)
                if dz % 2 == 0:
                    self.push(left, place(0, 1))
                self.push(left, place(0, 0, 1))
                self.arrive(right)
                if dz % 2 == 1:
                    self.push(right, place(0, -1))
                self.push(right, place(0, 0, 1))

        def far(self):
            for dz in range(4):
                piece = place(-dz, 2)
                self.arrive(piece)
                self.push(piece, place(0, 0, 1))

        def sibling(self):
            for dz in range(4):
                for dy in (0, -1, 1, 2):
                    self.arrive(place(-dz, dy, 1))

    o_gather = Gather(o_all, o_send, o_recv)
    u_gather = Gather(u_all, u_send, u_recv)

    plane, slot = lax.div(seat, 4), lax.rem(seat, 4)
    stays = plane == me
    swap = remote(
        out_weight,
        o_all.at[me * 4 + slot],
        o_swap.at[0],
        o_swap.at[1],
        (plane, me * 4 + slot),
    )

    @pl.when(jnp.logical_not(stays))
    def _():
        swap.start()

    @pl.when(stays)
    def _():
        o_all[seat] = out_weight[...]

    embed_pad[...] = jnp.zeros_like(embed_pad)
    embed_pad[0:VARS] = embed[...]
    for part in range(4):
        wide = 512 if part < 3 else 128
        rhs = weight[part * 512 : part * 512 + 512] if part < 3 else embed_pad[...]
        both = lax.dot_general(
            left_side[...], rhs, (((1,), (1,)), ((), ())), preferred_element_type=F32
        )
        for group in range(8):
            u_part[group, :, part * 512 : part * 512 + wide] = both[
                group * 16 : group * 16 + 16
            ].astype(BF16)
            table_out[group, :, part * 512 : part * 512 + wide] = both[
                128 + group * 4 : 132 + group * 4
            ]
    for dx in (1, 2, 3):
        target = lax.rem(x + dx, 4)
        go(
            u_part.at[pl.ds(target * 2, 2)],
            u_in_x.at[dx - 1],
            x_send.at[dx - 1],
            x_recv.at[dx - 1],
            (target * 2 + half, seat),
        )
    for step in range(1, 8):
        target = lax.rem(me + step, 8)
        go(
            table_out.at[target],
            table_in.at[step - 1],
            t_send.at[step - 1],
            t_recv.at[step - 1],
            (target, seat),
        )

    @pl.when(jnp.logical_not(stays))
    def _():
        swap.wait_recv()

    o_gather.own()

    for dx in (1, 2, 3):
        remote(
            u_part.at[pl.ds(0, 2)],
            u_in_x.at[dx - 1],
            x_send.at[dx - 1],
            x_recv.at[dx - 1],
            (me, seat),
        ).wait_recv()
    for which in range(2):
        u_mid[which] = (
            u_part[x * 2 + which].astype(F32)
            + u_in_x[0, which].astype(F32)
            + u_in_x[1, which].astype(F32)
            + u_in_x[2, which].astype(F32)
        ).astype(BF16)
    fold = []
    for which in range(2):
        target = slot * 8 + x * 2 + which
        itself = jnp.logical_and(plane == me, target == seat)
        copy = remote(
            u_mid.at[which],
            u_in_z.at[half],
            z_send.at[which],
            z_recv.at[half],
            (plane, target),
        )
        fold.append((itself, copy))

        @pl.when(jnp.logical_not(itself))
        def _():
            copy.start()

        @pl.when(itself)
        def _():
            u_in_z[half] = u_mid[which]

    for step in range(1, 8):
        remote(
            table_out.at[0],
            table_in.at[step - 1],
            t_send.at[step - 1],
            t_recv.at[step - 1],
            (me, seat),
        ).wait_recv()
    folded = table_out[me]
    for step in range(1, 8):
        folded = folded + table_in[step - 1]
    table[...] = folded
    diagonal = lax.div(iota((VAR_CHUNK, CHUNK), 1), PIX) == iota((VAR_CHUNK, CHUNK), 0)
    for chunk in range(ROWS // CHUNK):
        span = slice(chunk * CHUNK, chunk * CHUNK + CHUNK)
        block = jnp.concatenate(
            [
                jnp.where(diagonal, table[head : head + 1, span], 0.0)
                for head in range(HEADS_DEV)
            ],
            axis=0,
        )
        high = block.astype(BF16)
        low = (block - high.astype(F32)).astype(BF16)
        pair = jnp.dot(
            jnp.concatenate([high, low], axis=0), patches[span], preferred_element_type=F32
        )
        pair = pair[0:64] + pair[64:128]
        pick = iota((VAR_CHUNK, 128), 1) == iota((VAR_CHUNK, 128), 0) + chunk * VAR_CHUNK
        for head in range(HEADS_DEV):
            base = jnp.sum(
                jnp.where(pick, table[head : head + 1, ROWS:DEPTH], 0.0), axis=1, keepdims=True
            )
            scores[head, chunk * VAR_CHUNK : (chunk + 1) * VAR_CHUNK] = (
                pair[head * VAR_CHUNK : (head + 1) * VAR_CHUNK] + base
            )
    for head in range(HEADS_DEV):
        raised = jnp.exp(scores[head]) * mask[...]
        attention[head] = (raised / jnp.sum(raised, axis=0, keepdims=True)).astype(BF16)

    for source in range(2):
        away = jnp.logical_or(y * 2 + source != me, me * 4 + zlo != seat)

        @pl.when(away)
        def _():
            remote(
                u_mid.at[0],
                u_in_z.at[source],
                z_send.at[0],
                z_recv.at[source],
                (me, seat),
            ).wait_recv()

    u_all[seat] = (u_in_z[0].astype(F32) + u_in_z[1].astype(F32)).astype(BF16)
    u_gather.own()
    o_gather.line()

    spread = (lax.div(iota((CHUNK, VAR_CHUNK), 0), PIX) == iota((CHUNK, VAR_CHUNK), 1)).astype(
        BF16
    )
    for head in range(HEADS_DEV):
        for chunk in range(ROWS // CHUNK):
            span = slice(chunk * CHUNK, chunk * CHUNK + CHUNK)
            wide = jnp.dot(
                spread,
                attention[head, chunk * VAR_CHUNK : (chunk + 1) * VAR_CHUNK],
                preferred_element_type=F32,
            )
            weighted[head, span] = wide.astype(BF16) * patches[span]
        weighted[head, ROWS : ROWS + VARS] = attention[head]
        weighted[head, ROWS + VARS :] = jnp.zeros((DEPTH - ROWS - VARS, TOK), BF16)

    u_gather.line()
    u_gather.ring()
    u_gather.far()
    o_gather.ring()
    u_gather.sibling()

    for head in range(HEADS_DEV):
        columns = jnp.dot(
            u_all[head * 8 : head * 8 + 8].reshape(128, DEPTH),
            weighted[head],
            preferred_element_type=F32,
        )
        heads[me, :, head * 128 : head * 128 + 128] = columns.T.astype(BF16)

    right, left = lax.rem(x + 1, 4), lax.rem(x + 3, 4)
    across = lax.rem(x + 2, 4)
    other = 1 - half
    p_count = [0]

    def send_heads(src, target):
        go(
            src,
            src,
            p_send.at[p_count[0]],
            p_recv.at[p_count[0]],
            (target, seat),
        )
        p_count[0] += 1

    def heads_here(ref, index):
        remote(ref, ref, p_send.at[index], p_recv.at[index], (me, seat)).wait_recv()

    send_heads(heads.at[me], x * 2 + other)
    send_heads(heads.at[me], right * 2 + half)
    send_heads(heads.at[me], left * 2 + half)

    o_gather.far()
    o_gather.sibling()
    total[...] = jnp.broadcast_to(bias[...].astype(F32), total.shape)

    def add(block):
        for quarter in range(4):
            span = slice(quarter * 128, quarter * 128 + 128)
            total[:, span] += jnp.dot(
                heads[block], o_all[block * 4 + quarter], preferred_element_type=F32
            )

    low_rows, high_rows = pl.ds(0, 128), pl.ds(128, 128)
    add(me)
    partner = x * 2 + other
    heads_here(heads.at[partner], 0)
    send_heads(heads.at[partner], right * 2 + half)
    send_heads(heads.at[partner], left * 2 + half)
    add(partner)
    for turn in range(2):
        which = half if turn == 0 else other
        heads_here(heads.at[left * 2 + which], 1 + 2 * turn)
        send_heads(heads.at[left * 2 + which, low_rows], right * 2 + half)
        heads_here(heads.at[right * 2 + which], 2 + 2 * turn)
        send_heads(heads.at[right * 2 + which, high_rows], left * 2 + half)
        add(left * 2 + which)
        add(right * 2 + which)
    for turn in range(2):
        which = half if turn == 0 else other
        heads_here(heads.at[across * 2 + which, low_rows], 5 + 2 * turn)
        heads_here(heads.at[across * 2 + which, high_rows], 6 + 2 * turn)
        add(across * 2 + which)
    out[...] = total[...].astype(BF16)

    for copy in sent:
        copy.wait_send()

    @pl.when(jnp.logical_not(stays))
    def _():
        swap.wait_send()

    for itself, copy in fold:

        @pl.when(jnp.logical_not(itself))
        def _():
            copy.wait_send()


def local(
    patches, embed_weight, var_embed, key_query, var_mask, value_weight, out_weight, out_bias
):
    left_side = jnp.concatenate([value_weight[:, 0, :].T, key_query.T], axis=0)
    vmem = pl.BlockSpec(memory_space=pltpu.VMEM)
    sems = pltpu.SemaphoreType.DMA
    return pl.pallas_call(
        kernel,
        out_shape=jax.ShapeDtypeStruct((TOK, COLS), BF16),
        in_specs=[vmem] * 7,
        out_specs=vmem,
        scratch_shapes=[
            pltpu.VMEM((32, COLS, 128), BF16),
            pltpu.VMEM((32, 16, DEPTH), BF16),
            pltpu.VMEM((8, 4, DEPTH), F32),
            pltpu.VMEM((7, 4, DEPTH), F32),
            pltpu.VMEM((8, 16, DEPTH), BF16),
            pltpu.VMEM((3, 2, 16, DEPTH), BF16),
            pltpu.VMEM((2, 16, DEPTH), BF16),
            pltpu.VMEM((2, 16, DEPTH), BF16),
            pltpu.VMEM((128, COLS), BF16),
            pltpu.VMEM((4, DEPTH), F32),
            pltpu.VMEM((HEADS_DEV, VARS, TOK), F32),
            pltpu.VMEM((HEADS_DEV, VARS, TOK), BF16),
            pltpu.VMEM((HEADS_DEV, DEPTH, TOK), BF16),
            pltpu.VMEM((8, TOK, COLS), BF16),
            pltpu.VMEM((TOK, COLS), F32),
            sems((31 + 3,)),
            sems((32,)),
            sems((31 + 3,)),
            sems((32,)),
            sems((2,)),
            sems((7,)),
            sems((7,)),
            sems((3,)),
            sems((3,)),
            sems((2,)),
            sems((2,)),
            sems((9,)),
            sems((9,)),
        ],
        compiler_params=pltpu.CompilerParams(
            has_side_effects=True, vmem_limit_bytes=48 * 1024 * 1024
        ),
        cost_estimate=pl.CostEstimate(
            flops=2_000_000_000, bytes_accessed=4_000_000, transcendentals=100_000
        ),
        name="aggregate",
    )(
        patches.reshape(ROWS, TOK),
        embed_weight.reshape(ROWS, COLS),
        var_embed,
        left_side,
        var_mask.astype(F32).reshape(VARS, 1),
        out_weight,
        out_bias.reshape(1, COLS),
    )


def solution(mesh):
    placed = (
        P(None, None, "seq"),
        P(None, None, "var"),
        P(None, "var"),
        P("var", None),
        P(),
        P("var", "seq", None),
        P("var", "seq"),
        P("var"),
    )
    return jax.shard_map(
        local, mesh=mesh, in_specs=placed, out_specs=P("seq", "var"), check_vma=False
    )
```

```python
import jax
import jax.numpy as jnp
from jax import lax
from jax.experimental import pallas as pl
from jax.experimental.pallas import tpu as pltpu
from jax.sharding import PartitionSpec as P

MESH = pl.DeviceIdType.MESH
F32 = jnp.float32
BF16 = jnp.bfloat16
VARS, PIX, TOK = 96, 16, 256
ROWS = VARS * PIX
DEPTH = ROWS + 128
CHUNK = 256
VAR_CHUNK = CHUNK // PIX
HEADS_DEV = 8
COLS = 512


def iota(shape, dim):
    return lax.broadcasted_iota(jnp.int32, shape, dim)


def kernel(
    patches_hbm,
    weight_hbm,
    embed_hbm,
    query_hbm,
    value_hbm,
    out_weight,
    mask,
    bias,
    out,
    patches,
    weight,
    embed_pad,
    value,
    left_side,
    o_all,
    u_all,
    table_out,
    table_in,
    table_mid,
    table_far,
    table,
    u_part,
    u_in_x,
    u_mid,
    u_in_z,
    scores,
    attention,
    weighted,
    heads,
    part_out,
    part_in,
    total,
    l_sem,
    o_send,
    o_recv,
    u_send,
    u_recv,
    o_swap,
    t_send,
    t_recv,
    x_send,
    x_recv,
    z_send,
    z_recv,
    p_send,
    p_recv,
):
    me = lax.axis_index("var")
    seat = lax.axis_index("seq")
    x, half = lax.div(me, 2), lax.rem(me, 2)
    zlo, y, core = lax.div(seat, 8), lax.rem(lax.div(seat, 2), 4), lax.rem(seat, 2)
    lane = lax.rem(seat, 8)
    z = half * 4 + zlo

    def turned(dz, dy, dc=0):
        return (
            lax.rem(z + dz + 8, 8),
            lax.rem(y + dy + 4, 4),
            lax.rem(core + dc, 2),
        )

    def device(z2, y2, c2):
        return (x * 2 + lax.div(z2, 4), lax.rem(z2, 4) * 8 + y2 * 2 + c2)

    loads = [
        pltpu.make_async_copy(value_hbm, value, l_sem.at[0]),
        pltpu.make_async_copy(query_hbm, left_side.at[pl.ds(128, 32)], l_sem.at[1]),
        pltpu.make_async_copy(embed_hbm, embed_pad.at[pl.ds(0, VARS)], l_sem.at[2]),
    ]
    for part in range(3):
        span = pl.ds(part * 512, 512)
        loads.append(
            pltpu.make_async_copy(weight_hbm.at[span], weight.at[span], l_sem.at[3 + part])
        )
    loads.append(pltpu.make_async_copy(patches_hbm, patches, l_sem.at[6]))

    swaps = lax.div(y, 2) != half
    swap_to = (x * 2 + 1 - half, (3 - zlo) * 8 + lax.rem(y + 2, 4) * 2 + core)
    fold_seat = x * 8 + lane
    here = [
        jnp.logical_and(zlo * 2 + which == me, fold_seat == seat) for which in range(2)
    ]
    barrier = pltpu.get_barrier_semaphore()

    def greet(target):
        pl.semaphore_signal(barrier, inc=1, device_id=target, device_id_type=MESH)

    for dx in (1, 2, 3):
        greet((lax.rem(x + dx, 4) * 2 + half, seat))
    for dz in (4, 3, -3, 2, -2, 1, -1):
        greet(device(*turned(dz, 0)))
    for dy in (1, -1):
        greet(device(*turned(0, dy)))
    greet(device(*turned(0, 0, 1)))
    for which in range(2):

        @pl.when(jnp.logical_not(here[which]))
        def _():
            greet((zlo * 2 + which, fold_seat))

    @pl.when(swaps)
    def _():
        greet(swap_to)

    for copy in loads:
        copy.start()
    stay = pltpu.make_async_copy(out_weight, o_all.at[seat], l_sem.at[7])

    @pl.when(jnp.logical_not(swaps))
    def _():
        stay.start()

    def remote(src, dst, send, recv, target):
        return pltpu.make_async_remote_copy(
            src_ref=src,
            dst_ref=dst,
            send_sem=send,
            recv_sem=recv,
            device_id=target,
            device_id_type=MESH,
        )

    sent = []

    def go(*args):
        copy = remote(*args)
        copy.start()
        sent.append(copy)

    class Gather:
        def __init__(self, buf, send, recv, index, steps):
            self.buf, self.send, self.recv, self.count = buf, send, recv, 0
            self.index, self.steps = index, steps

        def push(self, spot, target):
            piece = self.index(*spot)
            go(
                self.buf.at[piece],
                self.buf.at[piece],
                self.send.at[self.count],
                self.recv.at[piece],
                device(*target),
            )
            self.count += 1

        def arrive(self, spot):
            piece = self.index(*spot)
            remote(
                self.buf.at[piece],
                self.buf.at[piece],
                self.send.at[0],
                self.recv.at[piece],
                (me, seat),
            ).wait_recv()

        def own(self):
            spot = turned(0, 0)
            for step in self.steps:
                self.push(spot, self.along(step))
            self.sides(spot)

        def along(self, step, dy=0, dc=0):
            spot = turned(step, dy, dc)
            if self.steps == (1, 2, 3):
                spot = (half * 4 + lax.rem(zlo + step + 4, 4),) + spot[1:]
            return spot

        def sides(self, spot):
            self.push(spot, turned(0, 1))
            self.push(spot, turned(0, -1))
            self.push(spot, turned(0, 0, 1))

        def line(self):
            for step in self.steps:
                spot = self.along(-step)
                self.arrive(spot)
                self.sides(spot)

        def ring_one(self, place):
            step = ((0,) + self.steps)[place]
            left, right = self.along(-step, -1), self.along(-step, 1)
            self.arrive(left)
            if place % 2 == 0:
                self.push(left, turned(0, 1))
            self.push(left, turned(0, 0, 1))
            self.arrive(right)
            if place % 2 == 1:
                self.push(right, turned(0, -1))
            self.push(right, turned(0, 0, 1))

        def ring(self):
            for place in range(len(self.steps) + 1):
                self.ring_one(place)

        def far(self):
            for step in (0,) + self.steps:
                spot = self.along(-step, 2)
                self.arrive(spot)
                self.push(spot, turned(0, 0, 1))

        def sibling(self, dy):
            for step in (0,) + self.steps:
                self.arrive(self.along(-step, dy, 1))

    o_gather = Gather(
        o_all,
        o_send,
        o_recv,
        lambda z2, y2, c2: lax.rem(z2, 4) * 8 + y2 * 2 + c2,
        (1, 2, 3),
    )
    u_gather = Gather(
        u_all,
        u_send,
        u_recv,
        lambda z2, y2, c2: (y2 * 2 + c2) * 8 + lax.rem(z2, 4) * 2 + lax.div(z2, 4),
        (1, -1, 2, -2, 3, -3, 4),
    )
    swap = remote(
        out_weight,
        o_all.at[(3 - zlo) * 8 + lax.rem(y + 2, 4) * 2 + core],
        o_swap.at[0],
        o_swap.at[1],
        swap_to,
    )

    embed_pad[VARS:] = jnp.zeros((128 - VARS, COLS), BF16)
    for copy in loads[:3]:
        copy.wait()
    left_side[0:128] = value[...].astype(F32).T.astype(BF16)
    for part in (3, 0, 1, 2):
        wide = 512 if part < 3 else 128
        if part < 3:
            loads[3 + part].wait()
            rhs = weight[part * 512 : part * 512 + 512]
        else:
            rhs = embed_pad[...]
        both = lax.dot_general(
            left_side[...], rhs, (((1,), (1,)), ((), ())), preferred_element_type=F32
        )
        for group in range(8):
            u_part[group, :, part * 512 : part * 512 + wide] = both[
                group * 16 : group * 16 + 16
            ].astype(BF16)
        for group in range(4):
            table_out[group, :, part * 512 : part * 512 + wide] = both[
                128 + group * 8 : 136 + group * 8
            ]

    pl.semaphore_wait(
        barrier, 15 - here[0].astype(jnp.int32) - here[1].astype(jnp.int32) + swaps.astype(jnp.int32)
    )

    for dx in (2, 1, 3):
        target = lax.rem(x + dx, 4)
        go(
            u_part.at[pl.ds(target * 2, 2)],
            u_in_x.at[dx - 1],
            x_send.at[dx - 1],
            x_recv.at[dx - 1],
            (target * 2 + half, seat),
        )

    @pl.when(swaps)
    def _():
        swap.start()

    for dx in (2, 1, 3):
        target = lax.rem(x + dx, 4)
        go(
            table_out.at[target],
            table_in.at[dx - 1],
            t_send.at[dx - 1],
            t_recv.at[dx - 1],
            (target * 2 + half, seat),
        )

    def landed(ref, send, recv):
        remote(ref, ref, send, recv, (me, seat)).wait_recv()

    for dx in (1, 3, 2):
        landed(u_in_x.at[dx - 1], x_send.at[0], x_recv.at[dx - 1])
    for which in range(2):
        u_mid[which] = (
            u_part[x * 2 + which].astype(F32)
            + u_in_x[0, which].astype(F32)
            + u_in_x[1, which].astype(F32)
            + u_in_x[2, which].astype(F32)
        ).astype(BF16)
    fold = []
    for which in range(2):
        copy = remote(
            u_mid.at[which],
            u_in_z.at[half],
            z_send.at[which],
            z_recv.at[half],
            (zlo * 2 + which, fold_seat),
        )
        fold.append(copy)

        @pl.when(jnp.logical_not(here[which]))
        def _():
            copy.start()

        @pl.when(here[which])
        def _():
            u_in_z[half] = u_mid[which]

    for dx in (1, 3, 2):
        landed(table_in.at[dx - 1], t_send.at[0], t_recv.at[dx - 1])
    table_mid[...] = table_out[x] + table_in[0] + table_in[1] + table_in[2]
    go(
        table_mid,
        table_far,
        t_send.at[3],
        t_recv.at[3],
        (x * 2 + 1 - half, seat),
    )

    @pl.when(swaps)
    def _():
        landed(o_all.at[seat], o_swap.at[0], o_swap.at[1])

    @pl.when(jnp.logical_not(swaps))
    def _():
        stay.wait()

    o_gather.own()

    loads[6].wait()
    landed(table_far, t_send.at[0], t_recv.at[3])
    table[...] = table_mid[...] + table_far[...]
    diagonal = lax.div(iota((VAR_CHUNK, CHUNK), 1), PIX) == iota((VAR_CHUNK, CHUNK), 0)
    stacked = HEADS_DEV * VAR_CHUNK
    for chunk in range(ROWS // CHUNK):
        span = slice(chunk * CHUNK, chunk * CHUNK + CHUNK)
        block = jnp.concatenate(
            [
                jnp.where(diagonal, table[head : head + 1, span], 0.0)
                for head in range(HEADS_DEV)
            ],
            axis=0,
        )
        high = block.astype(BF16)
        low = (block - high.astype(F32)).astype(BF16)
        pair = jnp.dot(
            jnp.concatenate([high, low], axis=0), patches[span], preferred_element_type=F32
        )
        pair = pair[0:stacked] + pair[stacked : 2 * stacked]
        pick = iota((VAR_CHUNK, 128), 1) == iota((VAR_CHUNK, 128), 0) + chunk * VAR_CHUNK
        for head in range(HEADS_DEV):
            base = jnp.sum(
                jnp.where(pick, table[head : head + 1, ROWS:DEPTH], 0.0), axis=1, keepdims=True
            )
            scores[head, chunk * VAR_CHUNK : (chunk + 1) * VAR_CHUNK] = (
                pair[head * VAR_CHUNK : (head + 1) * VAR_CHUNK] + base
            )
    spread = (lax.div(iota((CHUNK, VAR_CHUNK), 0), PIX) == iota((CHUNK, VAR_CHUNK), 1)).astype(
        BF16
    )

    def weigh(head):
        raised = jnp.exp(scores[head]) * mask[...]
        attention[head] = (raised / jnp.sum(raised, axis=0, keepdims=True)).astype(BF16)
        for chunk in range(ROWS // CHUNK):
            span = slice(chunk * CHUNK, chunk * CHUNK + CHUNK)
            wide = jnp.dot(
                spread,
                attention[head, chunk * VAR_CHUNK : (chunk + 1) * VAR_CHUNK],
                preferred_element_type=F32,
            )
            weighted[head, span] = wide.astype(BF16) * patches[span]
        weighted[head, ROWS : ROWS + VARS] = attention[head]
        weighted[head, ROWS + VARS :] = jnp.zeros((DEPTH - ROWS - VARS, TOK), BF16)

    for head in range(HEADS_DEV):
        weigh(head)

    for source in range(2):

        @pl.when(jnp.logical_not(here[source]))
        def _():
            landed(u_in_z.at[source], z_send.at[0], z_recv.at[source])

    u_all[lane * 8 + zlo * 2 + half] = (u_in_z[0].astype(F32) + u_in_z[1].astype(F32)).astype(
        BF16
    )
    u_gather.own()
    o_gather.line()
    u_gather.line()

    def project(dy, dc):
        head = lax.rem(y + dy + 4, 4) * 2 + lax.rem(core + dc, 2)
        columns = jnp.dot(
            u_all[pl.ds(head * 8, 8)].reshape(128, DEPTH),
            weighted[head],
            preferred_element_type=F32,
        )
        heads[:, pl.ds(pl.multiple_of(head * 128, 128), 128)] = columns.T.astype(BF16)

    project(0, 0)
    u_gather.ring()
    o_gather.ring()
    project(-1, 0)
    project(1, 0)
    u_gather.far()
    project(2, 0)
    for dy in (0, -1, 1, 2):
        u_gather.sibling(dy)
        project(dy, 1)
    o_gather.far()
    for dy in (0, -1, 1, 2):
        o_gather.sibling(dy)

    def partial(target, dst):
        near = target * 8 + half * 4
        far = (3 - target) * 8 + (1 - half) * 4
        for quarter in range(4):
            own_rows = jnp.dot(
                heads[:, pl.ds(pl.multiple_of(half * 512, 512), 512)],
                o_all[near + quarter],
                preferred_element_type=F32,
            )
            other_rows = jnp.dot(
                heads[:, pl.ds(pl.multiple_of(512 - half * 512, 512), 512)],
                o_all[far + quarter],
                preferred_element_type=F32,
            )
            dst[:, quarter * 128 : quarter * 128 + 128] = (own_rows + other_rows).astype(
                dst.dtype
            )

    for dx in (2, 1, 3):
        target = lax.rem(x + dx, 4)
        partial(target, part_out.at[dx - 1])
        go(
            part_out.at[dx - 1],
            part_in.at[dx - 1],
            p_send.at[dx - 1],
            p_recv.at[dx - 1],
            (target * 2 + half, seat),
        )
    partial(x, total)
    for dx in (1, 3, 2):
        landed(part_in.at[dx - 1], p_send.at[0], p_recv.at[dx - 1])
    out[...] = (
        total[...]
        + part_in[0].astype(F32)
        + part_in[1].astype(F32)
        + part_in[2].astype(F32)
        + bias[...].astype(F32)
    ).astype(BF16)

    for copy in sent:
        copy.wait_send()

    @pl.when(swaps)
    def _():
        swap.wait_send()

    for which in range(2):

        @pl.when(jnp.logical_not(here[which]))
        def _():
            fold[which].wait_send()


def local(
    patches, embed_weight, var_embed, key_query, var_mask, value_weight, out_weight, out_bias
):
    vmem = pl.BlockSpec(memory_space=pltpu.VMEM)
    hbm = pl.BlockSpec(memory_space=pl.ANY)
    sems = pltpu.SemaphoreType.DMA
    return pl.pallas_call(
        kernel,
        out_shape=jax.ShapeDtypeStruct((TOK, COLS), BF16),
        in_specs=[hbm] * 6 + [vmem] * 2,
        out_specs=vmem,
        scratch_shapes=[
            pltpu.VMEM((ROWS, TOK), BF16),
            pltpu.VMEM((ROWS, COLS), BF16),
            pltpu.VMEM((128, COLS), BF16),
            pltpu.VMEM((COLS, 128), BF16),
            pltpu.VMEM((160, COLS), BF16),
            pltpu.VMEM((32, COLS, 128), BF16),
            pltpu.VMEM((64, 16, DEPTH), BF16),
            pltpu.VMEM((4, 8, DEPTH), F32),
            pltpu.VMEM((3, 8, DEPTH), F32),
            pltpu.VMEM((8, DEPTH), F32),
            pltpu.VMEM((8, DEPTH), F32),
            pltpu.VMEM((8, DEPTH), F32),
            pltpu.VMEM((8, 16, DEPTH), BF16),
            pltpu.VMEM((3, 2, 16, DEPTH), BF16),
            pltpu.VMEM((2, 16, DEPTH), BF16),
            pltpu.VMEM((2, 16, DEPTH), BF16),
            pltpu.VMEM((HEADS_DEV, VARS, TOK), F32),
            pltpu.VMEM((HEADS_DEV, VARS, TOK), BF16),
            pltpu.VMEM((HEADS_DEV, DEPTH, TOK), BF16),
            pltpu.VMEM((TOK, 1024), BF16),
            pltpu.VMEM((3, TOK, COLS), BF16),
            pltpu.VMEM((3, TOK, COLS), BF16),
            pltpu.VMEM((TOK, COLS), F32),
            sems((8,)),
            sems((31,)),
            sems((32,)),
            sems((63,)),
            sems((64,)),
            sems((2,)),
            sems((4,)),
            sems((4,)),
            sems((3,)),
            sems((3,)),
            sems((2,)),
            sems((2,)),
            sems((3,)),
            sems((3,)),
        ],
        compiler_params=pltpu.CompilerParams(
            has_side_effects=True, collective_id=0, vmem_limit_bytes=56 * 1024 * 1024
        ),
        cost_estimate=pl.CostEstimate(
            flops=2_000_000_000, bytes_accessed=4_000_000, transcendentals=200_000
        ),
        name="aggregate",
    )(
        patches.reshape(ROWS, TOK),
        embed_weight.reshape(ROWS, COLS),
        var_embed,
        key_query.T,
        value_weight.reshape(COLS, 128),
        out_weight,
        var_mask.astype(F32).reshape(VARS, 1),
        out_bias.reshape(1, COLS),
    )


def solution(mesh):
    placed = (
        P(None, None, "seq"),
        P(None, None, "var"),
        P(None, "var"),
        P("var", None),
        P(),
        P("var", "seq", None),
        P("var", "seq"),
        P("var"),
    )
    return jax.shard_map(
        local, mesh=mesh, in_specs=placed, out_specs=P("seq", "var"), check_vma=False
    )
```

```python
import jax
import jax.numpy as jnp
from jax import lax
from jax.experimental import pallas as pl
from jax.experimental.pallas import tpu as pltpu
from jax.sharding import PartitionSpec as P

MESH = pl.DeviceIdType.MESH
F32 = jnp.float32
BF16 = jnp.bfloat16
VARS, PIX, TOK = 96, 16, 256
ROWS = VARS * PIX
DEPTH = ROWS + 128
CHUNK = 256
VAR_CHUNK = CHUNK // PIX
HEADS_DEV = 8
COLS = 512


def iota(shape, dim):
    return lax.broadcasted_iota(jnp.int32, shape, dim)


def kernel(
    patches_hbm,
    weight_hbm,
    embed_hbm,
    query_hbm,
    value_hbm,
    out_weight,
    mask,
    out,
    patches,
    weight,
    embed_pad,
    value,
    left_side,
    o_all,
    u_all,
    table_out,
    table_in,
    table_mid,
    table_far,
    table,
    u_part,
    u_in_x,
    u_mid,
    u_in_z,
    scores,
    attention,
    weighted,
    heads,
    part_out,
    part_in,
    total,
    l_sem,
    o_send,
    o_recv,
    u_send,
    u_recv,
    o_swap,
    t_send,
    t_recv,
    x_send,
    x_recv,
    z_send,
    z_recv,
    p_send,
    p_recv,
):
    me = lax.axis_index("var")
    seat = lax.axis_index("seq")
    x, half = lax.div(me, 2), lax.rem(me, 2)
    zlo, y, core = lax.div(seat, 8), lax.rem(lax.div(seat, 2), 4), lax.rem(seat, 2)
    lane = lax.rem(seat, 8)
    z = half * 4 + zlo

    def turned(dz, dy, dc=0):
        return (
            lax.rem(z + dz + 8, 8),
            lax.rem(y + dy + 4, 4),
            lax.rem(core + dc, 2),
        )

    def device(z2, y2, c2):
        return (x * 2 + lax.div(z2, 4), lax.rem(z2, 4) * 8 + y2 * 2 + c2)

    loads = [
        pltpu.make_async_copy(value_hbm, value, l_sem.at[0]),
        pltpu.make_async_copy(query_hbm, left_side.at[pl.ds(128, 32)], l_sem.at[1]),
        pltpu.make_async_copy(embed_hbm, embed_pad.at[pl.ds(0, VARS)], l_sem.at[2]),
    ]
    for part in range(3):
        span = pl.ds(part * 512, 512)
        loads.append(
            pltpu.make_async_copy(weight_hbm.at[span], weight.at[span], l_sem.at[3 + part])
        )
    loads.append(pltpu.make_async_copy(patches_hbm, patches, l_sem.at[6]))

    swaps = lax.div(y, 2) != half
    swap_to = (x * 2 + 1 - half, jnp.where(zlo < 2, 3, 0) * 8 + (3 - y) * 2 + core)
    fold_seat = x * 8 + lane
    here = [
        jnp.logical_and(zlo * 2 + which == me, fold_seat == seat) for which in range(2)
    ]
    barrier = pltpu.get_barrier_semaphore()

    def greet(target):
        pl.semaphore_signal(barrier, inc=1, device_id=target, device_id_type=MESH)

    for dx in (1, 2, 3):
        greet((lax.rem(x + dx, 4) * 2 + half, seat))
    for dz in (4, 1, -1):
        greet(device(*turned(dz, 0)))
    for dy in (1, -1):
        greet(device(*turned(0, dy)))
    greet(device(*turned(0, 0, 1)))
    for which in range(2):

        @pl.when(jnp.logical_not(here[which]))
        def _():
            greet((zlo * 2 + which, fold_seat))

    @pl.when(jnp.logical_and(swaps, lax.rem(zlo, 3) == 0))
    def _():
        for line in (3 - zlo, jnp.where(zlo == 0, 2, 1)):
            greet((x * 2 + 1 - half, line * 8 + (3 - y) * 2 + core))

    for copy in loads:
        copy.start()
    stay = pltpu.make_async_copy(out_weight, o_all.at[seat], l_sem.at[7])

    @pl.when(jnp.logical_not(swaps))
    def _():
        stay.start()

    def remote(src, dst, send, recv, target):
        return pltpu.make_async_remote_copy(
            src_ref=src,
            dst_ref=dst,
            send_sem=send,
            recv_sem=recv,
            device_id=target,
            device_id_type=MESH,
        )

    sent = []

    def go(*args):
        copy = remote(*args)
        copy.start()
        sent.append(copy)

    def push(buf, piece, send, recv, target):
        remote(buf.at[piece], buf.at[piece], send, recv.at[piece], device(*target)).start()

    def arrive(buf, piece, recv):
        remote(buf.at[piece], buf.at[piece], recv.at[piece], recv.at[piece], (me, seat)).wait_recv()

    class FoldedGather:
        steps = (1, -1, 2, -2, 3, -3, 4)

        def __init__(self):
            self.count = 0

        def index(self, z2, y2, c2):
            return (y2 * 2 + c2) * 8 + lax.rem(z2, 4) * 2 + lax.div(z2, 4)

        def push(self, spot, target):
            push(u_all, self.index(*spot), u_send.at[self.count], u_recv, target)
            self.count += 1

        def arrive(self, spot):
            arrive(u_all, self.index(*spot), u_recv)

        def sides(self, spot):
            self.push(spot, turned(0, 1))
            self.push(spot, turned(0, -1))
            self.push(spot, turned(0, 0, 1))

        def own(self):
            for sign in (1, -1):
                self.push(turned(0, 0), turned(sign, 0))
            self.sides(turned(0, 0))

        def line(self, distance):
            if distance < 3:
                for sign in (1, -1):
                    spot = turned(-sign * distance, 0)
                    self.arrive(spot)
                    self.push(spot, turned(sign, 0))
                    self.sides(spot)
                return
            for sign in (1, -1):
                self.arrive(turned(-3 * sign, 0))
            around = 1 - 2 * core
            self.push(turned(-3 * around, 0), turned(around, 0))
            for step in (3, -3, 4):
                if step == 4:
                    self.arrive(turned(4, 0))
                self.sides(turned(step, 0))

        def ring(self):
            for place, step in enumerate((0,) + self.steps):
                left, right = turned(-step, -1), turned(-step, 1)
                self.arrive(left)
                if place % 2 == 0:
                    self.push(left, turned(0, 1))
                self.push(left, turned(0, 0, 1))
                self.arrive(right)
                if place % 2 == 1:
                    self.push(right, turned(0, -1))
                self.push(right, turned(0, 0, 1))

        def far(self):
            for step in (0,) + self.steps:
                self.arrive(turned(-step, 2))
                self.push(turned(-step, 2), turned(0, 0, 1))

        def sibling(self, dy):
            for step in (0,) + self.steps:
                self.arrive(turned(-step, dy, 1))

        def finish(self):
            for count in range(self.count):
                landed_send(u_all.at[0], u_send.at[count])

    targets = [lax.rem(x + dx, 4) for dx in (2, 1, 3, 0)]

    class OutGather:
        def __init__(self):
            low_end = zlo < 2
            middle = jnp.logical_and(zlo > 0, zlo < 3)
            first, second = jnp.where(low_end, 0, 3), jnp.where(low_end, 1, 2)
            come = (first, second, 3 - first, 3 - second)
            twice, mirror = lax.rem(zlo + 2, 4), 3 - zlo
            near = (
                zlo + 1 - 2 * lax.rem(zlo, 2),
                jnp.where(middle, mirror, twice),
                jnp.where(middle, twice, mirror),
                zlo,
            )
            self.lines = [jnp.where(swaps, a, b) for a, b in zip(come, near)]
            self.pushed = []

        def spot(self, turn, dy, dc=0):
            y2, target = lax.rem(y + dy + 4, 4), targets[turn]
            near = (lax.div(y2, 2) == half).astype(jnp.int32)
            line = near * target + (1 - near) * (3 - target)
            return half * 4 + line, y2, lax.rem(core + dc, 2)

        def index(self, z2, y2, c2):
            return lax.rem(z2, 4) * 8 + y2 * 2 + c2

        def push(self, spot, target, when=None):
            slot = len(self.pushed)
            self.pushed.append(when)

            def start():
                push(o_all, self.index(*spot), o_send.at[slot], o_recv, target)

            if when is None:
                start()
            else:
                pl.when(when)(start)

        def arrive(self, spot):
            arrive(o_all, self.index(*spot), o_recv)

        def sides(self, spot, when=None):
            self.push(spot, turned(0, 1), when)
            self.push(spot, turned(0, -1), when)
            self.push(spot, turned(0, 0, 1), when)

        def own(self):
            mine, stays = turned(0, 0), jnp.logical_not(swaps)
            self.push(mine, turned(1, 0), jnp.logical_and(stays, zlo < 3))
            self.push(mine, turned(-1, 0), jnp.logical_and(stays, zlo > 0))
            self.sides(mine, stays)

        def serve(self, order):
            line = self.lines[order]
            spot = (half * 4 + line, y, core)
            when = swaps if order == 3 else None
            if when is None:
                self.arrive(spot)
            else:
                pl.when(when)(lambda: self.arrive(spot))
            up = jnp.where(swaps, line < 2, line < zlo)
            goes = jnp.where(up, zlo < 3, zlo > 0)
            if when is not None:
                goes = jnp.logical_and(goes, when)
            self.push(spot, turned(jnp.where(up, 1, -1), 0), goes)
            self.sides(spot, when)

        def ring(self, turn):
            left, right = self.spot(turn, -1), self.spot(turn, 1)
            self.arrive(left)
            if turn % 2 == 0:
                self.push(left, turned(0, 1))
            self.push(left, turned(0, 0, 1))
            self.arrive(right)
            if turn % 2 == 1:
                self.push(right, turned(0, -1))
            self.push(right, turned(0, 0, 1))

        def far(self, turn):
            spot = self.spot(turn, 2)
            self.arrive(spot)
            self.push(spot, turned(0, 0, 1))

        def sibling(self, turn):
            for dy in (0, -1, 1, 2):
                self.arrive(self.spot(turn, dy, 1))

        def finish(self):
            for slot, when in enumerate(self.pushed):
                if when is None:
                    landed_send(o_all.at[0], o_send.at[slot])
                else:
                    pl.when(when)(lambda: landed_send(o_all.at[0], o_send.at[slot]))

    def landed_send(ref, send):
        remote(ref, ref, send, send, (me, seat)).wait_send()

    o_gather = OutGather()
    u_gather = FoldedGather()
    swap_piece = (3 - zlo) * 8 + (3 - y) * 2 + core
    swap = remote(out_weight, o_all.at[swap_piece], o_swap.at[0], o_recv.at[swap_piece], swap_to)

    embed_pad[VARS:] = jnp.zeros((128 - VARS, COLS), BF16)
    for copy in loads[:3]:
        copy.wait()
    left_side[0:128] = value[...].astype(F32).T.astype(BF16)
    for part in (3, 0, 1, 2):
        wide = 512 if part < 3 else 128
        if part < 3:
            loads[3 + part].wait()
            rhs = weight[part * 512 : part * 512 + 512]
        else:
            rhs = embed_pad[...]
        both = lax.dot_general(
            left_side[...], rhs, (((1,), (1,)), ((), ())), preferred_element_type=F32
        )
        for group in range(8):
            u_part[group, :, part * 512 : part * 512 + wide] = both[
                group * 16 : group * 16 + 16
            ].astype(BF16)
        for group in range(4):
            table_out[group, :, part * 512 : part * 512 + wide] = both[
                128 + group * 8 : 136 + group * 8
            ]

    pl.semaphore_wait(
        barrier, 11 - here[0].astype(jnp.int32) - here[1].astype(jnp.int32) + swaps.astype(jnp.int32)
    )

    for dx in (2, 1, 3):
        target = lax.rem(x + dx, 4)
        go(
            u_part.at[pl.ds(target * 2, 2)],
            u_in_x.at[dx - 1],
            x_send.at[dx - 1],
            x_recv.at[dx - 1],
            (target * 2 + half, seat),
        )

    @pl.when(swaps)
    def _():
        swap.start()

    @pl.when(jnp.logical_not(swaps))
    def _():
        stay.wait()

    o_gather.own()

    def landed(ref, send, recv):
        remote(ref, ref, send, recv, (me, seat)).wait_recv()

    for dx in (1, 3, 2):
        landed(u_in_x.at[dx - 1], x_send.at[0], x_recv.at[dx - 1])
    for which in range(2):
        u_mid[which] = (
            u_part[x * 2 + which].astype(F32)
            + u_in_x[0, which].astype(F32)
            + u_in_x[1, which].astype(F32)
            + u_in_x[2, which].astype(F32)
        ).astype(BF16)
    fold = []
    for which in range(2):
        copy = remote(
            u_mid.at[which],
            u_in_z.at[half],
            z_send.at[which],
            z_recv.at[half],
            (zlo * 2 + which, fold_seat),
        )
        fold.append(copy)

        @pl.when(jnp.logical_not(here[which]))
        def _():
            copy.start()

        @pl.when(here[which])
        def _():
            u_in_z[half] = u_mid[which]

    for dx in (2, 1, 3):
        target = lax.rem(x + dx, 4)
        go(
            table_out.at[target],
            table_in.at[dx - 1],
            t_send.at[dx - 1],
            t_recv.at[dx - 1],
            (target * 2 + half, seat),
        )

    o_gather.serve(0)

    for dx in (1, 3, 2):
        landed(table_in.at[dx - 1], t_send.at[0], t_recv.at[dx - 1])
    table_mid[...] = table_out[x] + table_in[0] + table_in[1] + table_in[2]
    go(
        table_mid,
        table_far,
        t_send.at[3],
        t_recv.at[3],
        (x * 2 + 1 - half, seat),
    )

    for source in range(2):

        @pl.when(jnp.logical_not(here[source]))
        def _():
            landed(u_in_z.at[source], z_send.at[0], z_recv.at[source])

    u_all[lane * 8 + zlo * 2 + half] = (u_in_z[0].astype(F32) + u_in_z[1].astype(F32)).astype(
        BF16
    )
    u_gather.own()

    u_gather.line(1)
    o_gather.serve(1)
    u_gather.line(2)
    o_gather.serve(2)
    u_gather.line(3)
    o_gather.serve(3)

    loads[6].wait()
    landed(table_far, t_send.at[0], t_recv.at[3])
    table[...] = table_mid[...] + table_far[...]
    diagonal = lax.div(iota((VAR_CHUNK, CHUNK), 1), PIX) == iota((VAR_CHUNK, CHUNK), 0)
    stacked = HEADS_DEV * VAR_CHUNK
    for chunk in range(ROWS // CHUNK):
        span = slice(chunk * CHUNK, chunk * CHUNK + CHUNK)
        block = jnp.concatenate(
            [
                jnp.where(diagonal, table[head : head + 1, span], 0.0)
                for head in range(HEADS_DEV)
            ],
            axis=0,
        )
        high = block.astype(BF16)
        low = (block - high.astype(F32)).astype(BF16)
        pair = jnp.dot(
            jnp.concatenate([high, low], axis=0), patches[span], preferred_element_type=F32
        )
        pair = pair[0:stacked] + pair[stacked : 2 * stacked]
        pick = iota((VAR_CHUNK, 128), 1) == iota((VAR_CHUNK, 128), 0) + chunk * VAR_CHUNK
        for head in range(HEADS_DEV):
            base = jnp.sum(
                jnp.where(pick, table[head : head + 1, ROWS:DEPTH], 0.0), axis=1, keepdims=True
            )
            scores[head, chunk * VAR_CHUNK : (chunk + 1) * VAR_CHUNK] = (
                pair[head * VAR_CHUNK : (head + 1) * VAR_CHUNK] + base
            )
    spread = (lax.div(iota((CHUNK, VAR_CHUNK), 0), PIX) == iota((CHUNK, VAR_CHUNK), 1)).astype(
        BF16
    )

    flags = jnp.broadcast_to(mask[...].astype(F32).reshape(1, VARS), (VARS, VARS))
    keep = jnp.sum(
        jnp.where(iota((VARS, VARS), 0) == iota((VARS, VARS), 1), flags, 0.0),
        axis=1,
        keepdims=True,
    )

    def weigh(head):
        raised = jnp.exp(scores[head]) * keep
        attention[head] = (raised / jnp.sum(raised, axis=0, keepdims=True)).astype(BF16)
        for chunk in range(ROWS // CHUNK):
            span = slice(chunk * CHUNK, chunk * CHUNK + CHUNK)
            wide = jnp.dot(
                spread,
                attention[head, chunk * VAR_CHUNK : (chunk + 1) * VAR_CHUNK],
                preferred_element_type=F32,
            )
            weighted[head, span] = wide.astype(BF16) * patches[span]
        weighted[head, ROWS : ROWS + VARS] = attention[head]
        weighted[head, ROWS + VARS :] = jnp.zeros((DEPTH - ROWS - VARS, TOK), BF16)

    for head in range(HEADS_DEV):
        weigh(head)

    def project(dy, dc):
        head = lax.rem(y + dy + 4, 4) * 2 + lax.rem(core + dc, 2)
        columns = jnp.dot(
            u_all[pl.ds(head * 8, 8)].reshape(128, DEPTH),
            weighted[head],
            preferred_element_type=F32,
        )
        heads[:, pl.ds(pl.multiple_of(head * 128, 128), 128)] = columns.T.astype(BF16)

    project(0, 0)
    u_gather.ring()
    for turn in range(4):
        o_gather.ring(turn)
    project(-1, 0)
    project(1, 0)
    u_gather.far()
    project(2, 0)
    for dy in (0, -1, 1, 2):
        u_gather.sibling(dy)
        project(dy, 1)

    def partial(target, dst):
        near = target * 8 + half * 4
        far = (3 - target) * 8 + (1 - half) * 4 + 2
        for quarter in range(4):
            own_rows = jnp.dot(
                heads[:, pl.ds(pl.multiple_of(half * 512, 512), 512)],
                o_all[near + quarter],
                preferred_element_type=F32,
            )
            other_rows = jnp.dot(
                heads[:, pl.ds(pl.multiple_of(512 - half * 512, 512), 512)],
                o_all[far + quarter - 4 * (quarter // 2)],
                preferred_element_type=F32,
            )
            dst[:, quarter * 128 : quarter * 128 + 128] = (own_rows + other_rows).astype(
                dst.dtype
            )

    low_rows, high_rows = pl.ds(0, 128), pl.ds(128, 128)
    right, left = (targets[1] * 2 + half, seat), (targets[2] * 2 + half, seat)

    def pass_on(src, dst, slot, target):
        go(src, dst, p_send.at[slot], p_recv.at[slot], target)

    def block(turn, dst):
        o_gather.far(turn)
        o_gather.sibling(turn)
        partial(targets[turn], dst)

    block(0, part_out.at[0])
    pass_on(part_out.at[0, low_rows], part_in.at[0, low_rows], 0, right)
    pass_on(part_out.at[0, high_rows], part_in.at[0, high_rows], 1, left)
    block(1, part_out.at[1])
    pass_on(part_out.at[1, high_rows], part_in.at[1, high_rows], 2, right)
    block(2, part_out.at[2])
    pass_on(part_out.at[2, low_rows], part_in.at[2, low_rows], 3, left)
    landed(part_in.at[0, low_rows], p_send.at[0], p_recv.at[0])
    part_out[1, 0:128] = (
        part_out[1, 0:128].astype(F32) + part_in[0, 0:128].astype(F32)
    ).astype(BF16)
    pass_on(part_out.at[1, low_rows], part_in.at[1, low_rows], 4, right)
    landed(part_in.at[0, high_rows], p_send.at[0], p_recv.at[1])
    part_out[2, 128:256] = (
        part_out[2, 128:256].astype(F32) + part_in[0, 128:256].astype(F32)
    ).astype(BF16)
    pass_on(part_out.at[2, high_rows], part_in.at[2, high_rows], 5, left)
    block(3, total)
    landed(part_in.at[1, high_rows], p_send.at[0], p_recv.at[2])
    landed(part_in.at[2, low_rows], p_send.at[0], p_recv.at[3])
    landed(part_in.at[1, low_rows], p_send.at[0], p_recv.at[4])
    landed(part_in.at[2, high_rows], p_send.at[0], p_recv.at[5])
    out[...] = total[...] + part_in[1].astype(F32) + part_in[2].astype(F32)

    for copy in sent:
        copy.wait_send()
    o_gather.finish()
    u_gather.finish()

    @pl.when(swaps)
    def _():
        swap.wait_send()

    for which in range(2):

        @pl.when(jnp.logical_not(here[which]))
        def _():
            fold[which].wait_send()


def local(
    patches, embed_weight, var_embed, key_query, var_mask, value_weight, out_weight, out_bias
):
    vmem = pl.BlockSpec(memory_space=pltpu.VMEM)
    hbm = pl.BlockSpec(memory_space=pl.ANY)
    sems = pltpu.SemaphoreType.DMA
    summed = pl.pallas_call(
        kernel,
        out_shape=jax.ShapeDtypeStruct((TOK, COLS), F32),
        in_specs=[hbm] * 6 + [vmem],
        out_specs=vmem,
        scratch_shapes=[
            pltpu.VMEM((ROWS, TOK), BF16),
            pltpu.VMEM((ROWS, COLS), BF16),
            pltpu.VMEM((128, COLS), BF16),
            pltpu.VMEM((COLS, 128), BF16),
            pltpu.VMEM((160, COLS), BF16),
            pltpu.VMEM((32, COLS, 128), BF16),
            pltpu.VMEM((64, 16, DEPTH), BF16),
            pltpu.VMEM((4, 8, DEPTH), F32),
            pltpu.VMEM((3, 8, DEPTH), F32),
            pltpu.VMEM((8, DEPTH), F32),
            pltpu.VMEM((8, DEPTH), F32),
            pltpu.VMEM((8, DEPTH), F32),
            pltpu.VMEM((8, 16, DEPTH), BF16),
            pltpu.VMEM((3, 2, 16, DEPTH), BF16),
            pltpu.VMEM((2, 16, DEPTH), BF16),
            pltpu.VMEM((2, 16, DEPTH), BF16),
            pltpu.VMEM((HEADS_DEV, VARS, TOK), F32),
            pltpu.VMEM((HEADS_DEV, VARS, TOK), BF16),
            pltpu.VMEM((HEADS_DEV, DEPTH, TOK), BF16),
            pltpu.VMEM((TOK, 1024), BF16),
            pltpu.VMEM((3, TOK, COLS), BF16),
            pltpu.VMEM((3, TOK, COLS), BF16),
            pltpu.VMEM((TOK, COLS), F32),
            sems((8,)),
            sems((41,)),
            sems((32,)),
            sems((63,)),
            sems((64,)),
            sems((1,)),
            sems((4,)),
            sems((4,)),
            sems((3,)),
            sems((3,)),
            sems((2,)),
            sems((2,)),
            sems((6,)),
            sems((6,)),
        ],
        compiler_params=pltpu.CompilerParams(
            has_side_effects=True, collective_id=0, vmem_limit_bytes=56 * 1024 * 1024
        ),
        cost_estimate=pl.CostEstimate(
            flops=2_000_000_000, bytes_accessed=4_000_000, transcendentals=200_000
        ),
        name="aggregate",
    )(
        patches.reshape(ROWS, TOK),
        embed_weight.reshape(ROWS, COLS),
        var_embed,
        key_query.T,
        value_weight.reshape(COLS, 128),
        out_weight,
        var_mask,
    )
    return (summed + out_bias.astype(F32)[None, :]).astype(BF16)


def solution(mesh):
    placed = (
        P(None, None, "seq"),
        P(None, None, "var"),
        P(None, "var"),
        P("var", None),
        P(),
        P("var", "seq", None),
        P("var", "seq"),
        P("var"),
    )
    return jax.shard_map(
        local, mesh=mesh, in_specs=placed, out_specs=P("seq", "var"), check_vma=False
    )
```

```python
import jax
import jax.numpy as jnp
from jax import lax
from jax.experimental import pallas as pl
from jax.experimental.pallas import tpu as pltpu
from jax.sharding import PartitionSpec as P

MESH = pl.DeviceIdType.MESH
F32 = jnp.float32
BF16 = jnp.bfloat16
VARS, PIX, TOK = 96, 16, 256
ROWS = VARS * PIX
DEPTH = ROWS + 128
CHUNK = 256
VAR_CHUNK = CHUNK // PIX
HEADS_DEV = 8
COLS = 512


def iota(shape, dim):
    return lax.broadcasted_iota(jnp.int32, shape, dim)


def kernel(
    patches_hbm,
    weight_hbm,
    embed_hbm,
    query_hbm,
    value_hbm,
    out_weight,
    mask,
    bias,
    out,
    patches,
    weight,
    embed_pad,
    value,
    left_side,
    o_all,
    u_all,
    table_out,
    table_in,
    table_mid,
    table_far,
    table,
    u_part,
    u_in_x,
    u_mid,
    u_in_z,
    scores,
    attention,
    weighted,
    heads,
    part_out,
    part_in,
    total,
    l_sem,
    o_send,
    o_recv,
    o_near,
    u_send,
    u_recv,
    u_near,
    o_swap,
    t_sem,
    x_sem,
    z_send,
    z_recv,
    p_send,
    p_recv,
):
    me = lax.axis_index("var")
    seat = lax.axis_index("seq")
    x, half = lax.div(me, 2), lax.rem(me, 2)
    zlo, y, core = lax.div(seat, 8), lax.rem(lax.div(seat, 2), 4), lax.rem(seat, 2)
    lane = lax.rem(seat, 8)
    z = half * 4 + zlo

    def turned(dz, dy, dc=0):
        return (
            lax.rem(z + dz + 8, 8),
            lax.rem(y + dy + 4, 4),
            lax.rem(core + dc, 2),
        )

    def device(z2, y2, c2):
        return (x * 2 + lax.div(z2, 4), lax.rem(z2, 4) * 8 + y2 * 2 + c2)

    loads = [
        pltpu.make_async_copy(value_hbm, value, l_sem.at[0]),
        pltpu.make_async_copy(query_hbm, left_side.at[pl.ds(128, 32)], l_sem.at[1]),
        pltpu.make_async_copy(embed_hbm, embed_pad.at[pl.ds(0, VARS)], l_sem.at[2]),
    ]
    for part in range(3):
        span = pl.ds(part * 512, 512)
        loads.append(
            pltpu.make_async_copy(weight_hbm.at[span], weight.at[span], l_sem.at[3 + part])
        )
    loads.append(pltpu.make_async_copy(patches_hbm, patches, l_sem.at[6]))

    swaps = lax.div(y, 2) != half
    swap_to = (x * 2 + 1 - half, (3 - zlo) * 8 + (3 - y) * 2 + core)
    fold_seat = x * 8 + lane
    here = [
        jnp.logical_and(zlo * 2 + which == me, fold_seat == seat) for which in range(2)
    ]
    barrier = pltpu.get_barrier_semaphore()

    def greet(target):
        pl.semaphore_signal(barrier, inc=1, device_id=target, device_id_type=MESH)

    for dx in (1, 2, 3):
        greet((lax.rem(x + dx, 4) * 2 + half, seat))
    for dz in (4, 1, -1):
        greet(device(*turned(dz, 0)))
    pl.when(lax.rem(zlo, 3) == 0)(lambda: greet((me, jnp.where(zlo == 0, 2, 1) * 8 + lane)))
    pl.when(lax.rem(zlo, 3) > 0)(lambda: greet((me, lax.rem(zlo + 2, 4) * 8 + lane)))
    for dy in (1, -1):
        greet(device(*turned(0, dy)))
    greet(device(*turned(0, 0, 1)))
    for which in range(2):

        @pl.when(jnp.logical_not(here[which]))
        def _():
            greet((zlo * 2 + which, fold_seat))

    pl.when(lax.rem(zlo, 3) == 0)(lambda: greet((me, (3 - zlo) * 8 + lane)))
    pl.when(swaps)(lambda: greet(swap_to))

    for copy in loads:
        copy.start()
    stay = pltpu.make_async_copy(out_weight, o_all.at[seat], l_sem.at[7])

    @pl.when(jnp.logical_not(swaps))
    def _():
        stay.start()

    def remote(src, dst, send, recv, target):
        return pltpu.make_async_remote_copy(
            src_ref=src,
            dst_ref=dst,
            send_sem=send,
            recv_sem=recv,
            device_id=target,
            device_id_type=MESH,
        )

    def push(buf, piece, send, recv, target):
        remote(buf.at[piece], buf.at[piece], send, recv, device(*target)).start()

    def landed(ref, recv):
        remote(ref, ref, recv, recv, (me, seat)).wait_recv()

    def left(ref, send):
        remote(ref, ref, send, send, (me, seat)).wait_send()

    class FoldedGather:
        steps = (1, -1, 2, -2, 3, -3, 4)

        def index(self, z2, y2, c2):
            return (y2 * 2 + c2) * 8 + lax.rem(z2, 4) * 2 + lax.div(z2, 4)

        def push(self, spot, target):
            push(u_all, self.index(*spot), u_send.at[0], u_recv.at[spot[1] * 8 + spot[0]], target)

        def arrive(self, spot):
            landed(u_all.at[self.index(*spot)], u_recv.at[spot[1] * 8 + spot[0]])

        def near(self, spot):
            push(u_all, self.index(*spot), u_send.at[0], u_near.at[spot[1]], turned(0, 0, 1))

        def sides(self, spot):
            self.push(spot, turned(0, 1))
            self.push(spot, turned(0, -1))
            self.near(spot)

        def own(self):
            for sign in (1, -1):
                self.push(turned(0, 0), turned(sign, 0))
            self.sides(turned(0, 0))

        def line(self, distance):
            if distance < 3:
                for sign in (1, -1):
                    spot = turned(-sign * distance, 0)
                    self.arrive(spot)
                    self.push(spot, turned(sign, 0))
                    self.sides(spot)
                return
            for sign in (1, -1):
                self.arrive(turned(-3 * sign, 0))
            around = 1 - 2 * core
            self.push(turned(-3 * around, 0), turned(around, 0))
            for step in (3, -3, 4):
                if step == 4:
                    self.arrive(turned(4, 0))
                self.sides(turned(step, 0))

        def ring(self):
            for place, step in enumerate((0,) + self.steps):
                left, right = turned(-step, -1), turned(-step, 1)
                self.arrive(left)
                if place % 2 == 0:
                    self.push(left, turned(0, 1))
                self.near(left)
                self.arrive(right)
                if place % 2 == 1:
                    self.push(right, turned(0, -1))
                self.near(right)

        def far(self):
            for step in (0,) + self.steps:
                self.arrive(turned(-step, 2))
                self.near(turned(-step, 2))

        def sibling(self, dy):
            y2 = lax.rem(y + dy + 4, 4)
            landed(u_all.at[pl.ds((y2 * 2 + 1 - core) * 8, 8)], u_near.at[y2])

        def finish(self):
            left(u_all.at[pl.ds(0, 63)], u_send.at[0])

    targets = [lax.rem(x + dx, 4) for dx in (2, 1, 3, 0)]

    class OutGather:
        def __init__(self):
            middle = jnp.logical_and(zlo > 0, zlo < 3)
            twice, mirror = lax.rem(zlo + 2, 4), 3 - zlo
            self.lines = (
                zlo + 1 - 2 * lax.rem(zlo, 2),
                jnp.where(middle, mirror, twice),
                jnp.where(middle, twice, mirror),
            )

        def spot(self, turn, dy, dc=0):
            y2, target = lax.rem(y + dy + 4, 4), targets[turn]
            near = (lax.div(y2, 2) == half).astype(jnp.int32)
            line = near * target + (1 - near) * (3 - target)
            return half * 4 + line, y2, lax.rem(core + dc, 2)

        def index(self, z2, y2, c2):
            return lax.rem(z2, 4) * 8 + y2 * 2 + c2

        def push(self, spot, target, kind):
            recv = o_recv.at[lax.rem(spot[0], 4) * 4 + spot[1]]
            push(o_all, self.index(*spot), o_send.at[kind], recv, target)

        def arrive(self, spot):
            landed(o_all.at[self.index(*spot)], o_recv.at[lax.rem(spot[0], 4) * 4 + spot[1]])

        def near(self, spot):
            line = lax.rem(spot[0], 4)
            target = jnp.where(lax.div(spot[1], 2) == half, line, 3 - line)
            push(o_all, self.index(*spot), o_send.at[0], o_near.at[target], turned(0, 0, 1))

        def sides(self, spot):
            self.push(spot, turned(0, 1), 0)
            self.push(spot, turned(0, -1), 0)
            self.near(spot)

        def own(self):
            mine = turned(0, 0)
            for line in self.lines:
                self.push(mine, (half * 4 + line, y, core), 1)
            self.sides(mine)

        def serve(self, order, crossed):
            spot = (half * 4 + self.lines[order], y, core)

            @pl.when(swaps if crossed else jnp.logical_not(swaps))
            def _():
                self.arrive(spot)
                self.sides(spot)

        def ring(self, turn):
            prior, following = self.spot(turn, -1), self.spot(turn, 1)
            self.arrive(prior)
            if turn % 2 == 0:
                self.push(prior, turned(0, 1), 0)
            self.near(prior)
            self.arrive(following)
            if turn % 2 == 1:
                self.push(following, turned(0, -1), 0)
            self.near(following)

        def far(self, turn):
            spot = self.spot(turn, 2)
            self.arrive(spot)
            self.near(spot)

        def sibling(self, turn):
            landed(o_all.at[pl.ds(0, 4)], o_near.at[targets[turn]])

        def finish(self):
            left(o_all.at[pl.ds(0, 28)], o_send.at[0])
            left(o_all.at[pl.ds(0, 3)], o_send.at[1])

    o_gather = OutGather()
    u_gather = FoldedGather()
    swap_piece = (3 - zlo) * 8 + (3 - y) * 2 + core
    swap = remote(
        out_weight,
        o_all.at[swap_piece],
        o_swap.at[0],
        o_recv.at[(3 - zlo) * 4 + 3 - y],
        swap_to,
    )

    embed_pad[VARS:] = jnp.zeros((128 - VARS, COLS), BF16)
    for copy in loads[:3]:
        copy.wait()
    left_side[0:128] = value[...].astype(F32).T.astype(BF16)
    for part in (3, 0, 1, 2):
        wide = 512 if part < 3 else 128
        if part < 3:
            loads[3 + part].wait()
            rhs = weight[part * 512 : part * 512 + 512]
        else:
            rhs = embed_pad[...]
        both = lax.dot_general(
            left_side[...], rhs, (((1,), (1,)), ((), ())), preferred_element_type=F32
        )
        for group in range(8):
            u_part[group, :, part * 512 : part * 512 + wide] = both[
                group * 16 : group * 16 + 16
            ].astype(BF16)
        for group in range(4):
            table_out[group, :, part * 512 : part * 512 + wide] = both[
                128 + group * 8 : 136 + group * 8
            ]

    pl.semaphore_wait(
        barrier, 12 + (lax.rem(zlo, 3) == 0).astype(jnp.int32) - here[0].astype(jnp.int32) - here[1].astype(jnp.int32) + swaps.astype(jnp.int32)
    )

    for dx in (2, 1, 3):
        target = lax.rem(x + dx, 4)
        remote(
            u_part.at[pl.ds(target * 2, 2)],
            u_in_x.at[dx - 1],
            x_sem.at[0],
            x_sem.at[1],
            (target * 2 + half, seat),
        ).start()

    @pl.when(swaps)
    def _():
        swap.start()

    @pl.when(jnp.logical_not(swaps))
    def _():
        stay.wait()
        o_gather.own()

    landed(u_in_x, x_sem.at[1])
    for which in range(2):
        u_mid[which] = (
            u_part[x * 2 + which].astype(F32)
            + u_in_x[0, which].astype(F32)
            + u_in_x[1, which].astype(F32)
            + u_in_x[2, which].astype(F32)
        ).astype(BF16)
    fold = []
    for which in range(2):
        copy = remote(
            u_mid.at[which],
            u_in_z.at[half],
            z_send.at[which],
            z_recv.at[half],
            (zlo * 2 + which, fold_seat),
        )
        fold.append(copy)
        pl.when(jnp.logical_not(here[which]))(copy.start)

        @pl.when(here[which])
        def _():
            u_in_z[half] = u_mid[which]

    def table_start():
        for dx in (2, 1, 3):
            target = lax.rem(x + dx, 4)
            remote(
                table_out.at[target],
                table_in.at[dx - 1],
                t_sem.at[0],
                t_sem.at[1],
                (target * 2 + half, seat),
            ).start()

    table_copy = remote(
        table_mid, table_far, t_sem.at[2], t_sem.at[3], (x * 2 + 1 - half, seat)
    )

    def table_pass():
        landed(table_in, t_sem.at[1])
        table_mid[...] = table_out[x] + table_in[0] + table_in[1] + table_in[2]
        table_copy.start()

    def reduce_z():
        for source in range(2):

            @pl.when(jnp.logical_not(here[source]))
            def _():
                landed(u_in_z.at[source], z_recv.at[source])

        u_all[lane * 8 + zlo * 2 + half] = (
            u_in_z[0].astype(F32) + u_in_z[1].astype(F32)
        ).astype(BF16)

    def project(dy, dc):
        head = lax.rem(y + dy + 4, 4) * 2 + lax.rem(core + dc, 2)
        columns = jnp.dot(
            u_all[pl.ds(head * 8, 8)].reshape(128, DEPTH),
            weighted[head],
            preferred_element_type=F32,
        )
        heads[:, pl.ds(pl.multiple_of(head * 128, 128), 128)] = columns.T.astype(BF16)

    table_start()
    o_gather.serve(0, 0)
    reduce_z()
    u_gather.own()

    @pl.when(swaps)
    def _():
        o_gather.arrive(turned(0, 0))
        o_gather.own()

    o_gather.serve(1, 0)
    o_gather.serve(2, 0)
    table_pass()
    u_gather.line(1)
    o_gather.serve(0, 1)
    o_gather.serve(1, 1)
    u_gather.line(2)
    loads[6].wait()
    table_copy.wait_recv()
    table[...] = table_mid[...] + table_far[...]
    diagonal = lax.div(iota((VAR_CHUNK, CHUNK), 1), PIX) == iota((VAR_CHUNK, CHUNK), 0)
    stacked = HEADS_DEV * VAR_CHUNK
    for chunk in range(ROWS // CHUNK):
        span = slice(chunk * CHUNK, chunk * CHUNK + CHUNK)
        block = jnp.concatenate(
            [
                jnp.where(diagonal, table[head : head + 1, span], 0.0)
                for head in range(HEADS_DEV)
            ],
            axis=0,
        )
        high = block.astype(BF16)
        low = (block - high.astype(F32)).astype(BF16)
        pair = jnp.dot(
            jnp.concatenate([high, low], axis=0), patches[span], preferred_element_type=F32
        )
        pair = pair[0:stacked] + pair[stacked : 2 * stacked]
        pick = iota((VAR_CHUNK, 128), 1) == iota((VAR_CHUNK, 128), 0) + chunk * VAR_CHUNK
        for head in range(HEADS_DEV):
            base = jnp.sum(
                jnp.where(pick, table[head : head + 1, ROWS:DEPTH], 0.0), axis=1, keepdims=True
            )
            scores[head, chunk * VAR_CHUNK : (chunk + 1) * VAR_CHUNK] = (
                pair[head * VAR_CHUNK : (head + 1) * VAR_CHUNK] + base
            )
    spread = (lax.div(iota((CHUNK, VAR_CHUNK), 0), PIX) == iota((CHUNK, VAR_CHUNK), 1)).astype(
        BF16
    )

    flags = jnp.broadcast_to(mask[...].astype(F32).reshape(1, VARS), (VARS, VARS))
    keep = jnp.sum(
        jnp.where(iota((VARS, VARS), 0) == iota((VARS, VARS), 1), flags, 0.0),
        axis=1,
        keepdims=True,
    )

    def weigh(head):
        raised = jnp.exp(scores[head]) * keep
        attention[head] = (raised / jnp.sum(raised, axis=0, keepdims=True)).astype(BF16)
        for chunk in range(ROWS // CHUNK):
            span = slice(chunk * CHUNK, chunk * CHUNK + CHUNK)
            wide = jnp.dot(
                spread,
                attention[head, chunk * VAR_CHUNK : (chunk + 1) * VAR_CHUNK],
                preferred_element_type=F32,
            )
            weighted[head, span] = wide.astype(BF16) * patches[span]
        weighted[head, ROWS : ROWS + VARS] = attention[head]
        weighted[head, ROWS + VARS :] = jnp.zeros((DEPTH - ROWS - VARS, TOK), BF16)

    for head in range(HEADS_DEV):
        weigh(head)

    o_gather.serve(2, 1)
    u_gather.line(3)
    project(0, 0)
    u_gather.ring()
    o_gather.ring(0)
    o_gather.ring(1)
    o_gather.ring(2)
    o_gather.ring(3)
    project(-1, 0)
    project(1, 0)
    u_gather.sibling(0)
    project(0, 1)
    u_gather.sibling(-1)
    project(-1, 1)
    u_gather.sibling(1)
    project(1, 1)
    u_gather.far()
    project(2, 0)
    u_gather.sibling(2)
    project(2, 1)

    def partial(target, dst):
        near = target * 8 + half * 4
        far = (3 - target) * 8 + (1 - half) * 4 + 2
        for quarter in range(4):
            own_rows = jnp.dot(
                heads[:, pl.ds(pl.multiple_of(half * 512, 512), 512)],
                o_all[near + quarter],
                preferred_element_type=F32,
            )
            other_rows = jnp.dot(
                heads[:, pl.ds(pl.multiple_of(512 - half * 512, 512), 512)],
                o_all[far + quarter - 4 * (quarter // 2)],
                preferred_element_type=F32,
            )
            dst[:, quarter * 128 : quarter * 128 + 128] = (own_rows + other_rows).astype(
                dst.dtype
            )

    low_rows, high_rows = pl.ds(0, 128), pl.ds(128, 128)
    to_right, to_left = (targets[1] * 2 + half, seat), (targets[2] * 2 + half, seat)

    def pass_on(src, dst, slot, target):
        remote(src, dst, p_send.at[0], p_recv.at[slot], target).start()

    def block(turn, dst):
        o_gather.far(turn)
        o_gather.sibling(turn)
        partial(targets[turn], dst)

    block(0, part_out.at[0])
    pass_on(part_out.at[0, low_rows], part_in.at[0, low_rows], 0, to_right)
    pass_on(part_out.at[0, high_rows], part_in.at[0, high_rows], 1, to_left)
    block(1, part_out.at[1])
    pass_on(part_out.at[1, high_rows], part_in.at[1, high_rows], 2, to_right)
    block(2, part_out.at[2])
    pass_on(part_out.at[2, low_rows], part_in.at[2, low_rows], 3, to_left)
    landed(part_in.at[0, low_rows], p_recv.at[0])
    part_out[1, 0:128] = (
        part_out[1, 0:128].astype(F32) + part_in[0, 0:128].astype(F32)
    ).astype(BF16)
    pass_on(part_out.at[1, low_rows], part_in.at[1, low_rows], 4, to_right)
    landed(part_in.at[0, high_rows], p_recv.at[1])
    part_out[2, 128:256] = (
        part_out[2, 128:256].astype(F32) + part_in[0, 128:256].astype(F32)
    ).astype(BF16)
    pass_on(part_out.at[2, high_rows], part_in.at[2, high_rows], 5, to_left)
    block(3, total)
    landed(part_in.at[1, high_rows], p_recv.at[2])
    landed(part_in.at[2, low_rows], p_recv.at[3])
    landed(part_in.at[1, low_rows], p_recv.at[4])
    landed(part_in.at[2, high_rows], p_recv.at[5])
    offset = bias[...].astype(F32).reshape(1, COLS)
    out[...] = (
        total[...] + part_in[1].astype(F32) + part_in[2].astype(F32) + offset
    ).astype(BF16)

    o_gather.finish()
    u_gather.finish()
    left(u_in_x, x_sem.at[0])
    left(table_in, t_sem.at[0])
    table_copy.wait_send()
    left(part_out, p_send.at[0])
    pl.when(swaps)(swap.wait_send)
    for which in range(2):
        pl.when(jnp.logical_not(here[which]))(fold[which].wait_send)


def local(
    patches, embed_weight, var_embed, key_query, var_mask, value_weight, out_weight, out_bias
):
    vmem = pl.BlockSpec(memory_space=pltpu.VMEM)
    hbm = pl.BlockSpec(memory_space=pl.ANY)
    sems = pltpu.SemaphoreType.DMA
    return pl.pallas_call(
        kernel,
        out_shape=jax.ShapeDtypeStruct((TOK, COLS), BF16),
        in_specs=[hbm] * 6 + [vmem] * 2,
        out_specs=vmem,
        scratch_shapes=[
            pltpu.VMEM((ROWS, TOK), BF16),
            pltpu.VMEM((ROWS, COLS), BF16),
            pltpu.VMEM((128, COLS), BF16),
            pltpu.VMEM((COLS, 128), BF16),
            pltpu.VMEM((160, COLS), BF16),
            pltpu.VMEM((32, COLS, 128), BF16),
            pltpu.VMEM((64, 16, DEPTH), BF16),
            pltpu.VMEM((4, 8, DEPTH), F32),
            pltpu.VMEM((3, 8, DEPTH), F32),
            pltpu.VMEM((8, DEPTH), F32),
            pltpu.VMEM((8, DEPTH), F32),
            pltpu.VMEM((8, DEPTH), F32),
            pltpu.VMEM((8, 16, DEPTH), BF16),
            pltpu.VMEM((3, 2, 16, DEPTH), BF16),
            pltpu.VMEM((2, 16, DEPTH), BF16),
            pltpu.VMEM((2, 16, DEPTH), BF16),
            pltpu.VMEM((HEADS_DEV, VARS, TOK), F32),
            pltpu.VMEM((HEADS_DEV, VARS, TOK), BF16),
            pltpu.VMEM((HEADS_DEV, DEPTH, TOK), BF16),
            pltpu.VMEM((TOK, 1024), BF16),
            pltpu.VMEM((3, TOK, COLS), BF16),
            pltpu.VMEM((3, TOK, COLS), BF16),
            pltpu.VMEM((TOK, COLS), F32),
            sems((8,)),
            sems((2,)),
            sems((16,)),
            sems((4,)),
            sems((1,)),
            sems((32,)),
            sems((4,)),
            sems((1,)),
            sems((4,)),
            sems((2,)),
            sems((2,)),
            sems((2,)),
            sems((1,)),
            sems((6,)),
        ],
        compiler_params=pltpu.CompilerParams(
            has_side_effects=True, collective_id=0, vmem_limit_bytes=56 * 1024 * 1024
        ),
        cost_estimate=pl.CostEstimate(
            flops=2_000_000_000, bytes_accessed=4_000_000, transcendentals=200_000
        ),
        name="aggregate",
    )(
        patches.reshape(ROWS, TOK),
        embed_weight.reshape(ROWS, COLS),
        var_embed,
        key_query.T,
        value_weight.reshape(COLS, 128),
        out_weight,
        var_mask,
        out_bias,
    )


def solution(mesh):
    placed = (
        P(None, None, "seq"),
        P(None, None, "var"),
        P(None, "var"),
        P("var", None),
        P(),
        P("var", "seq", None),
        P("var", "seq"),
        P("var"),
    )
    return jax.shard_map(
        local, mesh=mesh, in_specs=placed, out_specs=P("seq", "var"), check_vma=False
    )
```

```python
import jax
import jax.numpy as jnp
from jax import lax
from jax.experimental import pallas as pl
from jax.experimental.pallas import tpu as pltpu
from jax.sharding import PartitionSpec as P

MESH = pl.DeviceIdType.MESH
F32 = jnp.float32
BF16 = jnp.bfloat16
VARS, PIX, TOK = 96, 16, 256
ROWS = VARS * PIX
DEPTH = ROWS + 128
CHUNK = 256
VAR_CHUNK = CHUNK // PIX
HEADS_DEV = 8
COLS = 512


def iota(shape, dim):
    return lax.broadcasted_iota(jnp.int32, shape, dim)


def kernel(
    patches_hbm,
    weight_hbm,
    embed_hbm,
    query_hbm,
    value_hbm,
    out_weight,
    mask_hbm,
    bias_hbm,
    out,
    mask,
    bias,
    patches,
    weight,
    embed_pad,
    value,
    left_side,
    o_all,
    u_all,
    table_out,
    table_in,
    table_mid,
    table_far,
    table,
    u_part,
    u_in_x,
    u_mid,
    u_in_z,
    scores,
    attention,
    weighted,
    heads,
    part_out,
    part_in,
    total,
    l_sem,
    o_send,
    o_recv,
    o_near,
    u_send,
    u_recv,
    u_near,
    o_swap,
    t_sem,
    x_sem,
    z_send,
    z_recv,
    p_send,
    p_recv,
):
    me = lax.axis_index("var")
    seat = lax.axis_index("seq")
    x, half = lax.div(me, 2), lax.rem(me, 2)
    zlo, y, core = lax.div(seat, 8), lax.rem(lax.div(seat, 2), 4), lax.rem(seat, 2)
    lane = lax.rem(seat, 8)
    z = half * 4 + zlo

    def turned(dz, dy, dc=0):
        return (
            lax.rem(z + dz + 8, 8),
            lax.rem(y + dy + 4, 4),
            lax.rem(core + dc, 2),
        )

    def device(z2, y2, c2):
        return (x * 2 + lax.div(z2, 4), lax.rem(z2, 4) * 8 + y2 * 2 + c2)

    loads = [
        pltpu.make_async_copy(value_hbm, value, l_sem.at[0]),
        pltpu.make_async_copy(query_hbm, left_side.at[pl.ds(128, 32)], l_sem.at[1]),
        pltpu.make_async_copy(embed_hbm, embed_pad.at[pl.ds(0, VARS)], l_sem.at[2]),
    ]
    weight_loads = []
    for part in range(6):
        span = pl.ds(part * 256, 256)
        weight_loads.append(
            pltpu.make_async_copy(weight_hbm.at[span], weight.at[span], l_sem.at[10 + part])
        )
    loads.append(pltpu.make_async_copy(patches_hbm, patches, l_sem.at[6]))
    loads.append(pltpu.make_async_copy(mask_hbm, mask, l_sem.at[8]))
    loads.append(pltpu.make_async_copy(bias_hbm, bias, l_sem.at[9]))

    swaps = lax.div(y, 2) != half
    swap_to = (x * 2 + 1 - half, (3 - zlo) * 8 + (3 - y) * 2 + core)
    fold_seat = x * 8 + lane
    here = [
        jnp.logical_and(zlo * 2 + which == me, fold_seat == seat) for which in range(2)
    ]
    barrier = pltpu.get_barrier_semaphore()

    def greet(target):
        pl.semaphore_signal(barrier, inc=1, device_id=target, device_id_type=MESH)

    for dx in (1, 2, 3):
        greet((lax.rem(x + dx, 4) * 2 + half, seat))
    for dz in (4, 1, -1):
        greet(device(*turned(dz, 0)))
    pl.when(lax.rem(zlo, 3) == 0)(lambda: greet((me, jnp.where(zlo == 0, 2, 1) * 8 + lane)))
    pl.when(lax.rem(zlo, 3) > 0)(lambda: greet((me, lax.rem(zlo + 2, 4) * 8 + lane)))
    for dy in (1, -1):
        greet(device(*turned(0, dy)))
    greet(device(*turned(0, 0, 1)))
    for which in range(2):

        @pl.when(jnp.logical_not(here[which]))
        def _():
            greet((zlo * 2 + which, fold_seat))

    pl.when(lax.rem(zlo, 3) == 0)(lambda: greet((me, (3 - zlo) * 8 + lane)))
    pl.when(swaps)(lambda: greet(swap_to))

    for copy in loads[:3] + weight_loads + loads[3:]:
        copy.start()
    stay = pltpu.make_async_copy(out_weight, o_all.at[seat], l_sem.at[7])

    @pl.when(jnp.logical_not(swaps))
    def _():
        stay.start()

    def remote(src, dst, send, recv, target):
        return pltpu.make_async_remote_copy(
            src_ref=src,
            dst_ref=dst,
            send_sem=send,
            recv_sem=recv,
            device_id=target,
            device_id_type=MESH,
        )

    def push(buf, piece, send, recv, target):
        remote(buf.at[piece], buf.at[piece], send, recv, device(*target)).start()

    def landed(ref, recv):
        remote(ref, ref, recv, recv, (me, seat)).wait_recv()

    def left(ref, send):
        remote(ref, ref, send, send, (me, seat)).wait_send()

    class FoldedGather:
        steps = (1, -1, 2, -2, 3, -3, 4)

        def index(self, z2, y2, c2):
            return (y2 * 2 + c2) * 8 + lax.rem(z2, 4) * 2 + lax.div(z2, 4)

        def push(self, spot, target):
            push(u_all, self.index(*spot), u_send.at[0], u_recv.at[spot[1] * 8 + spot[0]], target)

        def arrive(self, spot):
            landed(u_all.at[self.index(*spot)], u_recv.at[spot[1] * 8 + spot[0]])

        def near(self, spot):
            push(u_all, self.index(*spot), u_send.at[0], u_near.at[spot[1]], turned(0, 0, 1))

        def sides(self, spot):
            self.push(spot, turned(0, 1))
            self.push(spot, turned(0, -1))
            self.near(spot)

        def own(self):
            for sign in (1, -1):
                self.push(turned(0, 0), turned(sign, 0))
            self.sides(turned(0, 0))

        def line(self, distance):
            if distance < 3:
                for sign in (1, -1):
                    spot = turned(-sign * distance, 0)
                    self.arrive(spot)
                    self.push(spot, turned(sign, 0))
                    self.sides(spot)
                return
            for sign in (1, -1):
                self.arrive(turned(-3 * sign, 0))
            around = 1 - 2 * core
            self.push(turned(-3 * around, 0), turned(around, 0))
            for step in (3, -3, 4):
                if step == 4:
                    self.arrive(turned(4, 0))
                self.sides(turned(step, 0))

        def ring(self):
            for place, step in enumerate((0,) + self.steps):
                left, right = turned(-step, -1), turned(-step, 1)
                self.arrive(left)
                if place % 2 == 0:
                    self.push(left, turned(0, 1))
                self.near(left)
                self.arrive(right)
                if place % 2 == 1:
                    self.push(right, turned(0, -1))
                self.near(right)

        def far(self):
            for step in (0,) + self.steps:
                self.arrive(turned(-step, 2))
                self.near(turned(-step, 2))

        def sibling(self, dy):
            y2 = lax.rem(y + dy + 4, 4)
            landed(u_all.at[pl.ds((y2 * 2 + 1 - core) * 8, 8)], u_near.at[y2])

        def finish(self):
            left(u_all.at[pl.ds(0, 63)], u_send.at[0])

    targets = [lax.rem(x + dx, 4) for dx in (2, 1, 3, 0)]

    class OutGather:
        def __init__(self):
            middle = jnp.logical_and(zlo > 0, zlo < 3)
            twice, mirror = lax.rem(zlo + 2, 4), 3 - zlo
            self.lines = (
                zlo + 1 - 2 * lax.rem(zlo, 2),
                jnp.where(middle, mirror, twice),
                jnp.where(middle, twice, mirror),
            )

        def spot(self, turn, dy, dc=0):
            y2, target = lax.rem(y + dy + 4, 4), targets[turn]
            near = (lax.div(y2, 2) == half).astype(jnp.int32)
            line = near * target + (1 - near) * (3 - target)
            return half * 4 + line, y2, lax.rem(core + dc, 2)

        def index(self, z2, y2, c2):
            return lax.rem(z2, 4) * 8 + y2 * 2 + c2

        def push(self, spot, target, kind):
            recv = o_recv.at[lax.rem(spot[0], 4) * 4 + spot[1]]
            push(o_all, self.index(*spot), o_send.at[kind], recv, target)

        def arrive(self, spot):
            landed(o_all.at[self.index(*spot)], o_recv.at[lax.rem(spot[0], 4) * 4 + spot[1]])

        def near(self, spot):
            line = lax.rem(spot[0], 4)
            target = jnp.where(lax.div(spot[1], 2) == half, line, 3 - line)
            push(o_all, self.index(*spot), o_send.at[0], o_near.at[target], turned(0, 0, 1))

        def sides(self, spot):
            self.push(spot, turned(0, 1), 0)
            self.push(spot, turned(0, -1), 0)
            self.near(spot)

        def own(self):
            mine = turned(0, 0)
            for line in self.lines:
                self.push(mine, (half * 4 + line, y, core), 1)
            self.sides(mine)

        def serve(self, order, crossed):
            spot = (half * 4 + self.lines[order], y, core)

            @pl.when(swaps if crossed else jnp.logical_not(swaps))
            def _():
                self.arrive(spot)
                self.sides(spot)

        def ring(self, turn):
            prior, following = self.spot(turn, -1), self.spot(turn, 1)
            self.arrive(prior)
            if turn % 2 == 0:
                self.push(prior, turned(0, 1), 0)
            self.near(prior)
            self.arrive(following)
            if turn % 2 == 1:
                self.push(following, turned(0, -1), 0)
            self.near(following)

        def far(self, turn):
            spot = self.spot(turn, 2)
            self.arrive(spot)
            self.near(spot)

        def sibling(self, turn):
            landed(o_all.at[pl.ds(0, 4)], o_near.at[targets[turn]])

        def finish(self):
            left(o_all.at[pl.ds(0, 28)], o_send.at[0])
            left(o_all.at[pl.ds(0, 3)], o_send.at[1])

    o_gather = OutGather()
    u_gather = FoldedGather()
    swap_piece = (3 - zlo) * 8 + (3 - y) * 2 + core
    swap = remote(
        out_weight,
        o_all.at[swap_piece],
        o_swap.at[0],
        o_recv.at[(3 - zlo) * 4 + 3 - y],
        swap_to,
    )

    embed_pad[VARS:] = jnp.zeros((128 - VARS, COLS), BF16)
    for copy in loads[:3]:
        copy.wait()
    left_side[0:128] = value[...].astype(F32).T.astype(BF16)
    for part in (3, 0, 1, 2):
        wide = 512 if part < 3 else 128
        if part < 3:
            weight_loads[2 * part].wait()
            weight_loads[2 * part + 1].wait()
            rhs = weight[part * 512 : part * 512 + 512]
        else:
            rhs = embed_pad[...]
        both = lax.dot_general(
            left_side[...], rhs, (((1,), (1,)), ((), ())), preferred_element_type=F32
        )
        for group in range(8):
            u_part[group, :, part * 512 : part * 512 + wide] = both[
                group * 16 : group * 16 + 16
            ].astype(BF16)
        for group in range(4):
            table_out[group, :, part * 512 : part * 512 + wide] = both[
                128 + group * 8 : 136 + group * 8
            ]

    pl.semaphore_wait(
        barrier, 12 + (lax.rem(zlo, 3) == 0).astype(jnp.int32) - here[0].astype(jnp.int32) - here[1].astype(jnp.int32) + swaps.astype(jnp.int32)
    )

    for dx in (2, 1, 3):
        target = lax.rem(x + dx, 4)
        remote(
            u_part.at[pl.ds(target * 2, 2)],
            u_in_x.at[dx - 1],
            x_sem.at[0],
            x_sem.at[1],
            (target * 2 + half, seat),
        ).start()

    @pl.when(swaps)
    def _():
        swap.start()

    @pl.when(jnp.logical_not(swaps))
    def _():
        stay.wait()
        o_gather.own()

    landed(u_in_x, x_sem.at[1])
    for which in range(2):
        u_mid[which] = (
            u_part[x * 2 + which].astype(F32)
            + u_in_x[0, which].astype(F32)
            + u_in_x[1, which].astype(F32)
            + u_in_x[2, which].astype(F32)
        ).astype(BF16)
    fold = []
    for which in range(2):
        copy = remote(
            u_mid.at[which],
            u_in_z.at[half],
            z_send.at[which],
            z_recv.at[half],
            (zlo * 2 + which, fold_seat),
        )
        fold.append(copy)
        pl.when(jnp.logical_not(here[which]))(copy.start)

        @pl.when(here[which])
        def _():
            u_in_z[half] = u_mid[which]

    first_core = core == 0
    table_copy = remote(
        table_mid, table_far, t_sem.at[2], t_sem.at[3], (x * 2 + 1 - half, seat)
    )
    table_share = remote(
        table, table, t_sem.at[4], t_sem.at[5], device(*turned(0, 0, 1))
    )

    def table_start():
        @pl.when(first_core)
        def _():
            for dx in (2, 1, 3):
                target = lax.rem(x + dx, 4)
                remote(
                    table_out.at[target],
                    table_in.at[dx - 1],
                    t_sem.at[0],
                    t_sem.at[1],
                    (target * 2 + half, seat),
                ).start()

    def table_pass():
        @pl.when(first_core)
        def _():
            landed(table_in, t_sem.at[1])
            table_mid[...] = table_out[x] + table_in[0] + table_in[1] + table_in[2]
            table_copy.start()

    def table_end():
        @pl.when(first_core)
        def _():
            table_copy.wait_recv()
            table[...] = table_mid[...] + table_far[...]
            table_share.start()

        pl.when(jnp.logical_not(first_core))(table_share.wait_recv)

    def reduce_z():
        for source in range(2):

            @pl.when(jnp.logical_not(here[source]))
            def _():
                landed(u_in_z.at[source], z_recv.at[source])

        u_all[lane * 8 + zlo * 2 + half] = (
            u_in_z[0].astype(F32) + u_in_z[1].astype(F32)
        ).astype(BF16)

    def project(dy, dc):
        head = lax.rem(y + dy + 4, 4) * 2 + lax.rem(core + dc, 2)
        columns = jnp.dot(
            u_all[pl.ds(head * 8, 8)].reshape(128, DEPTH),
            weighted[head],
            preferred_element_type=F32,
        )
        heads[:, pl.ds(pl.multiple_of(head * 128, 128), 128)] = columns.T.astype(BF16)

    table_start()
    o_gather.serve(0, 0)
    reduce_z()
    u_gather.own()

    @pl.when(swaps)
    def _():
        o_gather.arrive(turned(0, 0))
        o_gather.own()

    o_gather.serve(1, 0)
    o_gather.serve(2, 0)
    u_gather.line(1)
    table_pass()
    o_gather.serve(0, 1)
    o_gather.serve(1, 1)
    u_gather.line(2)
    for copy in loads[3:]:
        copy.wait()
    table_end()
    diagonal = lax.div(iota((VAR_CHUNK, CHUNK), 1), PIX) == iota((VAR_CHUNK, CHUNK), 0)
    stacked = HEADS_DEV * VAR_CHUNK
    for chunk in range(ROWS // CHUNK):
        span = slice(chunk * CHUNK, chunk * CHUNK + CHUNK)
        block = jnp.concatenate(
            [
                jnp.where(diagonal, table[head : head + 1, span], 0.0)
                for head in range(HEADS_DEV)
            ],
            axis=0,
        )
        high = block.astype(BF16)
        low = (block - high.astype(F32)).astype(BF16)
        pair = jnp.dot(
            jnp.concatenate([high, low], axis=0), patches[span], preferred_element_type=F32
        )
        pair = pair[0:stacked] + pair[stacked : 2 * stacked]
        pick = iota((VAR_CHUNK, 128), 1) == iota((VAR_CHUNK, 128), 0) + chunk * VAR_CHUNK
        for head in range(HEADS_DEV):
            base = jnp.sum(
                jnp.where(pick, table[head : head + 1, ROWS:DEPTH], 0.0), axis=1, keepdims=True
            )
            scores[head, chunk * VAR_CHUNK : (chunk + 1) * VAR_CHUNK] = (
                pair[head * VAR_CHUNK : (head + 1) * VAR_CHUNK] + base
            )
    spread = (lax.div(iota((CHUNK, VAR_CHUNK), 0), PIX) == iota((CHUNK, VAR_CHUNK), 1)).astype(
        BF16
    )

    flags = jnp.broadcast_to(mask[...].astype(F32).reshape(1, VARS), (VARS, VARS))
    keep = jnp.sum(
        jnp.where(iota((VARS, VARS), 0) == iota((VARS, VARS), 1), flags, 0.0),
        axis=1,
        keepdims=True,
    )

    def weigh(head):
        raised = jnp.exp(scores[head]) * keep
        attention[head] = (raised / jnp.sum(raised, axis=0, keepdims=True)).astype(BF16)
        for chunk in range(ROWS // CHUNK):
            span = slice(chunk * CHUNK, chunk * CHUNK + CHUNK)
            wide = jnp.dot(
                spread,
                attention[head, chunk * VAR_CHUNK : (chunk + 1) * VAR_CHUNK],
                preferred_element_type=F32,
            )
            weighted[head, span] = wide.astype(BF16) * patches[span]
        weighted[head, ROWS : ROWS + VARS] = attention[head]
        weighted[head, ROWS + VARS :] = jnp.zeros((DEPTH - ROWS - VARS, TOK), BF16)

    for head in range(HEADS_DEV):
        weigh(head)

    o_gather.serve(2, 1)
    u_gather.line(3)
    project(0, 0)
    u_gather.ring()
    o_gather.ring(0)
    o_gather.ring(1)
    o_gather.ring(2)
    o_gather.ring(3)
    project(-1, 0)
    project(1, 0)
    u_gather.sibling(0)
    project(0, 1)
    u_gather.sibling(-1)
    project(-1, 1)
    u_gather.sibling(1)
    project(1, 1)
    u_gather.far()
    project(2, 0)
    u_gather.sibling(2)
    project(2, 1)

    def partial(target, dst):
        near = target * 8 + half * 4
        far = (3 - target) * 8 + (1 - half) * 4 + 2
        for quarter in range(4):
            own_rows = jnp.dot(
                heads[:, pl.ds(pl.multiple_of(half * 512, 512), 512)],
                o_all[near + quarter],
                preferred_element_type=F32,
            )
            other_rows = jnp.dot(
                heads[:, pl.ds(pl.multiple_of(512 - half * 512, 512), 512)],
                o_all[far + quarter - 4 * (quarter // 2)],
                preferred_element_type=F32,
            )
            dst[:, quarter * 128 : quarter * 128 + 128] = (own_rows + other_rows).astype(
                dst.dtype
            )

    low_rows, high_rows = pl.ds(0, 128), pl.ds(128, 128)
    to_right, to_left = (targets[1] * 2 + half, seat), (targets[2] * 2 + half, seat)

    def pass_on(src, dst, slot, target):
        remote(src, dst, p_send.at[0], p_recv.at[slot], target).start()

    def block(turn, dst):
        o_gather.far(turn)
        o_gather.sibling(turn)
        partial(targets[turn], dst)

    block(0, part_out.at[0])
    pass_on(part_out.at[0, low_rows], part_in.at[0, low_rows], 0, to_right)
    pass_on(part_out.at[0, high_rows], part_in.at[0, high_rows], 1, to_left)
    block(1, part_out.at[1])
    pass_on(part_out.at[1, high_rows], part_in.at[1, high_rows], 2, to_right)
    block(2, part_out.at[2])
    pass_on(part_out.at[2, low_rows], part_in.at[2, low_rows], 3, to_left)
    landed(part_in.at[0, low_rows], p_recv.at[0])
    part_out[1, 0:128] = (
        part_out[1, 0:128].astype(F32) + part_in[0, 0:128].astype(F32)
    ).astype(BF16)
    pass_on(part_out.at[1, low_rows], part_in.at[1, low_rows], 4, to_right)
    landed(part_in.at[0, high_rows], p_recv.at[1])
    part_out[2, 128:256] = (
        part_out[2, 128:256].astype(F32) + part_in[0, 128:256].astype(F32)
    ).astype(BF16)
    pass_on(part_out.at[2, high_rows], part_in.at[2, high_rows], 5, to_left)
    block(3, total)
    landed(part_in.at[1, high_rows], p_recv.at[2])
    landed(part_in.at[2, low_rows], p_recv.at[3])
    landed(part_in.at[1, low_rows], p_recv.at[4])
    landed(part_in.at[2, high_rows], p_recv.at[5])
    offset = bias[...].astype(F32).reshape(1, COLS)
    out[...] = (
        total[...] + part_in[1].astype(F32) + part_in[2].astype(F32) + offset
    ).astype(BF16)

    o_gather.finish()
    u_gather.finish()
    left(u_in_x, x_sem.at[0])

    @pl.when(first_core)
    def _():
        left(table_in, t_sem.at[0])
        table_copy.wait_send()
        table_share.wait_send()

    left(part_out, p_send.at[0])
    pl.when(swaps)(swap.wait_send)
    for which in range(2):
        pl.when(jnp.logical_not(here[which]))(fold[which].wait_send)


def local(
    patches, embed_weight, var_embed, key_query, var_mask, value_weight, out_weight, out_bias
):
    vmem = pl.BlockSpec(memory_space=pltpu.VMEM)
    hbm = pl.BlockSpec(memory_space=pl.ANY)
    sems = pltpu.SemaphoreType.DMA
    return pl.pallas_call(
        kernel,
        out_shape=jax.ShapeDtypeStruct((TOK, COLS), BF16),
        in_specs=[hbm] * 8,
        out_specs=vmem,
        scratch_shapes=[
            pltpu.VMEM((VARS,), jnp.int32),
            pltpu.VMEM((COLS,), BF16),
            pltpu.VMEM((ROWS, TOK), BF16),
            pltpu.VMEM((ROWS, COLS), BF16),
            pltpu.VMEM((128, COLS), BF16),
            pltpu.VMEM((COLS, 128), BF16),
            pltpu.VMEM((160, COLS), BF16),
            pltpu.VMEM((32, COLS, 128), BF16),
            pltpu.VMEM((64, 16, DEPTH), BF16),
            pltpu.VMEM((4, 8, DEPTH), F32),
            pltpu.VMEM((3, 8, DEPTH), F32),
            pltpu.VMEM((8, DEPTH), F32),
            pltpu.VMEM((8, DEPTH), F32),
            pltpu.VMEM((8, DEPTH), F32),
            pltpu.VMEM((8, 16, DEPTH), BF16),
            pltpu.VMEM((3, 2, 16, DEPTH), BF16),
            pltpu.VMEM((2, 16, DEPTH), BF16),
            pltpu.VMEM((2, 16, DEPTH), BF16),
            pltpu.VMEM((HEADS_DEV, VARS, TOK), F32),
            pltpu.VMEM((HEADS_DEV, VARS, TOK), BF16),
            pltpu.VMEM((HEADS_DEV, DEPTH, TOK), BF16),
            pltpu.VMEM((TOK, 1024), BF16),
            pltpu.VMEM((3, TOK, COLS), BF16),
            pltpu.VMEM((3, TOK, COLS), BF16),
            pltpu.VMEM((TOK, COLS), F32),
            sems((16,)),
            sems((2,)),
            sems((16,)),
            sems((4,)),
            sems((1,)),
            sems((32,)),
            sems((4,)),
            sems((1,)),
            sems((6,)),
            sems((2,)),
            sems((2,)),
            sems((2,)),
            sems((1,)),
            sems((6,)),
        ],
        compiler_params=pltpu.CompilerParams(
            has_side_effects=True, collective_id=0, vmem_limit_bytes=56 * 1024 * 1024
        ),
        cost_estimate=pl.CostEstimate(
            flops=2_000_000_000, bytes_accessed=4_000_000, transcendentals=200_000
        ),
        name="aggregate",
    )(
        patches.reshape(ROWS, TOK),
        embed_weight.reshape(ROWS, COLS),
        var_embed,
        key_query.T,
        value_weight.reshape(COLS, 128),
        out_weight,
        var_mask,
        out_bias,
    )


def solution(mesh):
    placed = (
        P(None, None, "seq"),
        P(None, None, "var"),
        P(None, "var"),
        P("var", None),
        P(),
        P("var", "seq", None),
        P("var", "seq"),
        P("var"),
    )
    return jax.shard_map(
        local, mesh=mesh, in_specs=placed, out_specs=P("seq", "var"), check_vma=False
    )
```

```python
import jax
import jax.numpy as jnp
from jax import lax
from jax.experimental import pallas as pl
from jax.experimental.pallas import tpu as pltpu
from jax.sharding import PartitionSpec as P

MESH = pl.DeviceIdType.MESH
F32 = jnp.float32
BF16 = jnp.bfloat16
VARS, PIX, TOK = 96, 16, 256
ROWS = VARS * PIX
DEPTH = ROWS + 128
CHUNK = 256
VAR_CHUNK = CHUNK // PIX
HEADS_DEV = 8
COLS = 512


def iota(shape, dim):
    return lax.broadcasted_iota(jnp.int32, shape, dim)


def kernel(
    patches_hbm,
    weight_hbm,
    embed_hbm,
    query_hbm,
    value_hbm,
    out_weight,
    mask_hbm,
    bias_hbm,
    out,
    mask,
    bias,
    patches,
    weight,
    embed_pad,
    value,
    left_side,
    o_all,
    u_all,
    table_out,
    table_in,
    table_mid,
    table_far,
    table,
    u_part,
    u_in_x,
    u_mid,
    u_in_z,
    scores,
    attention,
    weighted,
    heads,
    part_out,
    part_in,
    total,
    l_sem,
    o_send,
    o_recv,
    o_near,
    u_send,
    u_recv,
    u_near,
    o_swap,
    t_sem,
    x_sem,
    z_send,
    z_recv,
    p_send,
    p_recv,
):
    me = lax.axis_index("var")
    seat = lax.axis_index("seq")
    x, half = lax.div(me, 2), lax.rem(me, 2)
    zlo, y, core = lax.div(seat, 8), lax.rem(lax.div(seat, 2), 4), lax.rem(seat, 2)
    lane = lax.rem(seat, 8)
    z = half * 4 + zlo

    def turned(dz, dy, dc=0):
        return (
            lax.rem(z + dz + 8, 8),
            lax.rem(y + dy + 4, 4),
            lax.rem(core + dc, 2),
        )

    def device(z2, y2, c2):
        return (x * 2 + lax.div(z2, 4), lax.rem(z2, 4) * 8 + y2 * 2 + c2)

    loads = [
        pltpu.make_async_copy(value_hbm, value, l_sem.at[0]),
        pltpu.make_async_copy(query_hbm, left_side.at[pl.ds(128, 32)], l_sem.at[1]),
        pltpu.make_async_copy(embed_hbm, embed_pad.at[pl.ds(0, VARS)], l_sem.at[2]),
    ]
    weight_loads = []
    for part in range(6):
        span = pl.ds(part * 256, 256)
        weight_loads.append(
            pltpu.make_async_copy(weight_hbm.at[span], weight.at[span], l_sem.at[10 + part])
        )
    loads.append(pltpu.make_async_copy(patches_hbm, patches, l_sem.at[6]))
    loads.append(pltpu.make_async_copy(mask_hbm, mask, l_sem.at[8]))
    loads.append(pltpu.make_async_copy(bias_hbm, bias, l_sem.at[9]))

    swaps = lax.div(y, 2) != half
    swap_to = (x * 2 + 1 - half, (3 - zlo) * 8 + (3 - y) * 2 + core)
    fold_seat = x * 8 + lane
    here = [
        jnp.logical_and(zlo * 2 + which == me, fold_seat == seat) for which in range(2)
    ]
    barrier = pltpu.get_barrier_semaphore()

    def greet(target):
        pl.semaphore_signal(barrier, inc=1, device_id=target, device_id_type=MESH)

    for dx in (1, 2, 3):
        greet((lax.rem(x + dx, 4) * 2 + half, seat))
    for dz in (4, 1, -1):
        greet(device(*turned(dz, 0)))
    pl.when(lax.rem(zlo, 3) == 0)(lambda: greet((me, jnp.where(zlo == 0, 2, 1) * 8 + lane)))
    pl.when(lax.rem(zlo, 3) > 0)(lambda: greet((me, lax.rem(zlo + 2, 4) * 8 + lane)))
    for dy in (1, -1):
        greet(device(*turned(0, dy)))
    greet(device(*turned(0, 0, 1)))
    for which in range(2):

        @pl.when(jnp.logical_not(here[which]))
        def _():
            greet((zlo * 2 + which, fold_seat))

    pl.when(lax.rem(zlo, 3) == 0)(lambda: greet((me, (3 - zlo) * 8 + lane)))
    pl.when(swaps)(lambda: greet(swap_to))

    for copy in loads[:3] + weight_loads + loads[3:]:
        copy.start()
    stay = pltpu.make_async_copy(out_weight, o_all.at[seat], l_sem.at[7])

    @pl.when(jnp.logical_not(swaps))
    def _():
        stay.start()

    def remote(src, dst, send, recv, target):
        return pltpu.make_async_remote_copy(
            src_ref=src,
            dst_ref=dst,
            send_sem=send,
            recv_sem=recv,
            device_id=target,
            device_id_type=MESH,
        )

    def push(buf, piece, send, recv, target):
        remote(buf.at[piece], buf.at[piece], send, recv, device(*target)).start()

    def landed(ref, recv):
        remote(ref, ref, recv, recv, (me, seat)).wait_recv()

    def left(ref, send):
        remote(ref, ref, send, send, (me, seat)).wait_send()

    class FoldedGather:
        steps = (1, -1, 2, -2, 3, -3, 4)

        def index(self, z2, y2, c2):
            return (y2 * 2 + c2) * 8 + lax.rem(z2, 4) * 2 + lax.div(z2, 4)

        def push(self, spot, target):
            push(u_all, self.index(*spot), u_send.at[0], u_recv.at[spot[1] * 8 + spot[0]], target)

        def arrive(self, spot):
            landed(u_all.at[self.index(*spot)], u_recv.at[spot[1] * 8 + spot[0]])

        def near(self, spot):
            push(u_all, self.index(*spot), u_send.at[0], u_near.at[spot[1]], turned(0, 0, 1))

        def sides(self, spot):
            self.push(spot, turned(0, 1))
            self.push(spot, turned(0, -1))
            self.near(spot)

        def own(self):
            for sign in (1, -1):
                self.push(turned(0, 0), turned(sign, 0))
            self.sides(turned(0, 0))

        def line(self, distance):
            if distance < 3:
                for sign in (1, -1):
                    spot = turned(-sign * distance, 0)
                    self.arrive(spot)
                    self.push(spot, turned(sign, 0))
                    self.sides(spot)
                return
            for sign in (1, -1):
                self.arrive(turned(-3 * sign, 0))
            around = 1 - 2 * core
            self.push(turned(-3 * around, 0), turned(around, 0))
            for step in (3, -3, 4):
                if step == 4:
                    self.arrive(turned(4, 0))
                self.sides(turned(step, 0))

        def ring(self):
            for place, step in enumerate((0,) + self.steps):
                left, right = turned(-step, -1), turned(-step, 1)
                self.arrive(left)
                if place % 2 == 0:
                    self.push(left, turned(0, 1))
                self.near(left)
                self.arrive(right)
                if place % 2 == 1:
                    self.push(right, turned(0, -1))
                self.near(right)

        def far(self):
            for step in (0,) + self.steps:
                self.arrive(turned(-step, 2))
                self.near(turned(-step, 2))

        def sibling(self, dy):
            y2 = lax.rem(y + dy + 4, 4)
            landed(u_all.at[pl.ds((y2 * 2 + 1 - core) * 8, 8)], u_near.at[y2])

        def finish(self):
            left(u_all.at[pl.ds(0, 63)], u_send.at[0])

    targets = [lax.rem(x + dx, 4) for dx in (2, 1, 3, 0)]

    class OutGather:
        def __init__(self):
            middle = jnp.logical_and(zlo > 0, zlo < 3)
            twice, mirror = lax.rem(zlo + 2, 4), 3 - zlo
            self.lines = (
                zlo + 1 - 2 * lax.rem(zlo, 2),
                jnp.where(middle, mirror, twice),
                jnp.where(middle, twice, mirror),
            )

        def spot(self, turn, dy, dc=0):
            y2, target = lax.rem(y + dy + 4, 4), targets[turn]
            near = (lax.div(y2, 2) == half).astype(jnp.int32)
            line = near * target + (1 - near) * (3 - target)
            return half * 4 + line, y2, lax.rem(core + dc, 2)

        def index(self, z2, y2, c2):
            return lax.rem(z2, 4) * 8 + y2 * 2 + c2

        def push(self, spot, target, kind):
            recv = o_recv.at[lax.rem(spot[0], 4) * 4 + spot[1]]
            push(o_all, self.index(*spot), o_send.at[kind], recv, target)

        def arrive(self, spot):
            landed(o_all.at[self.index(*spot)], o_recv.at[lax.rem(spot[0], 4) * 4 + spot[1]])

        def near(self, spot):
            line = lax.rem(spot[0], 4)
            target = jnp.where(lax.div(spot[1], 2) == half, line, 3 - line)
            push(o_all, self.index(*spot), o_send.at[0], o_near.at[target], turned(0, 0, 1))

        def sides(self, spot):
            self.push(spot, turned(0, 1), 0)
            self.push(spot, turned(0, -1), 0)
            self.near(spot)

        def own(self):
            mine = turned(0, 0)
            for line in self.lines:
                self.push(mine, (half * 4 + line, y, core), 1)
            self.sides(mine)

        def serve(self, order, crossed):
            spot = (half * 4 + self.lines[order], y, core)

            @pl.when(swaps if crossed else jnp.logical_not(swaps))
            def _():
                self.arrive(spot)
                self.sides(spot)

        def ring(self, turn):
            prior, following = self.spot(turn, -1), self.spot(turn, 1)
            self.arrive(prior)
            if turn % 2 == 0:
                self.push(prior, turned(0, 1), 0)
            self.near(prior)
            self.arrive(following)
            if turn % 2 == 1:
                self.push(following, turned(0, -1), 0)
            self.near(following)

        def far(self, turn):
            spot = self.spot(turn, 2)
            self.arrive(spot)
            self.near(spot)

        def sibling(self, turn):
            landed(o_all.at[pl.ds(0, 4)], o_near.at[targets[turn]])

        def finish(self):
            left(o_all.at[pl.ds(0, 28)], o_send.at[0])
            left(o_all.at[pl.ds(0, 3)], o_send.at[1])

    o_gather = OutGather()
    u_gather = FoldedGather()
    swap_piece = (3 - zlo) * 8 + (3 - y) * 2 + core
    swap = remote(
        out_weight,
        o_all.at[swap_piece],
        o_swap.at[0],
        o_recv.at[(3 - zlo) * 4 + 3 - y],
        swap_to,
    )

    embed_pad[VARS:] = jnp.zeros((128 - VARS, COLS), BF16)
    for copy in loads[:3]:
        copy.wait()
    left_side[0:128] = value[...].astype(F32).T.astype(BF16)
    for part in (3, 0, 1, 2):
        wide = 512 if part < 3 else 128
        if part < 3:
            weight_loads[2 * part].wait()
            weight_loads[2 * part + 1].wait()
            rhs = weight[part * 512 : part * 512 + 512]
        else:
            rhs = embed_pad[...]
        both = lax.dot_general(
            left_side[...], rhs, (((1,), (1,)), ((), ())), preferred_element_type=F32
        )
        for group in range(8):
            u_part[group, :, part * 512 : part * 512 + wide] = both[
                group * 16 : group * 16 + 16
            ].astype(BF16)
        for group in range(4):
            table_out[group, :, part * 512 : part * 512 + wide] = both[
                128 + group * 8 : 136 + group * 8
            ]

    pl.semaphore_wait(
        barrier, 12 + (lax.rem(zlo, 3) == 0).astype(jnp.int32) - here[0].astype(jnp.int32) - here[1].astype(jnp.int32) + swaps.astype(jnp.int32)
    )

    for dx in (2, 1, 3):
        target = lax.rem(x + dx, 4)
        remote(
            u_part.at[pl.ds(target * 2, 2)],
            u_in_x.at[dx - 1],
            x_sem.at[0],
            x_sem.at[1],
            (target * 2 + half, seat),
        ).start()

    @pl.when(swaps)
    def _():
        swap.start()

    @pl.when(jnp.logical_not(swaps))
    def _():
        stay.wait()
        o_gather.own()

    landed(u_in_x, x_sem.at[1])
    for which in range(2):
        u_mid[which] = (
            u_part[x * 2 + which].astype(F32)
            + u_in_x[0, which].astype(F32)
            + u_in_x[1, which].astype(F32)
            + u_in_x[2, which].astype(F32)
        ).astype(BF16)
    fold = []
    for which in range(2):
        copy = remote(
            u_mid.at[which],
            u_in_z.at[half],
            z_send.at[which],
            z_recv.at[half],
            (zlo * 2 + which, fold_seat),
        )
        fold.append(copy)
        pl.when(jnp.logical_not(here[which]))(copy.start)

        @pl.when(here[which])
        def _():
            u_in_z[half] = u_mid[which]

    first_core = core == 0
    table_copy = remote(
        table_mid, table_far, t_sem.at[2], t_sem.at[3], (x * 2 + 1 - half, seat)
    )
    table_share = remote(
        table, table, t_sem.at[4], t_sem.at[5], device(*turned(0, 0, 1))
    )

    def table_start():
        @pl.when(first_core)
        def _():
            for dx in (2, 1, 3):
                target = lax.rem(x + dx, 4)
                remote(
                    table_out.at[target],
                    table_in.at[dx - 1],
                    t_sem.at[0],
                    t_sem.at[1],
                    (target * 2 + half, seat),
                ).start()

    def table_pass():
        @pl.when(first_core)
        def _():
            landed(table_in, t_sem.at[1])
            table_mid[...] = table_out[x] + table_in[0] + table_in[1] + table_in[2]
            table_copy.start()

    def table_end():
        @pl.when(first_core)
        def _():
            table_copy.wait_recv()
            table[...] = table_mid[...] + table_far[...]
            table_share.start()

        pl.when(jnp.logical_not(first_core))(table_share.wait_recv)

    def reduce_z():
        for source in range(2):

            @pl.when(jnp.logical_not(here[source]))
            def _():
                landed(u_in_z.at[source], z_recv.at[source])

        u_all[lane * 8 + zlo * 2 + half] = (
            u_in_z[0].astype(F32) + u_in_z[1].astype(F32)
        ).astype(BF16)

    def project(dy, dc):
        head = lax.rem(y + dy + 4, 4) * 2 + lax.rem(core + dc, 2)
        columns = jnp.dot(
            u_all[pl.ds(head * 8, 8)].reshape(128, DEPTH),
            weighted[head],
            preferred_element_type=F32,
        )
        heads[:, pl.ds(pl.multiple_of(head * 128, 128), 128)] = columns.T.astype(BF16)

    o_gather.serve(0, 0)
    table_start()
    o_gather.serve(1, 0)
    reduce_z()
    u_gather.own()

    @pl.when(swaps)
    def _():
        o_gather.arrive(turned(0, 0))
        o_gather.own()

    o_gather.serve(2, 0)
    u_gather.line(1)
    table_pass()
    o_gather.serve(0, 1)
    o_gather.serve(1, 1)
    u_gather.line(2)
    for copy in loads[3:]:
        copy.wait()
    table_end()
    diagonal = lax.div(iota((VAR_CHUNK, CHUNK), 1), PIX) == iota((VAR_CHUNK, CHUNK), 0)
    stacked = HEADS_DEV * VAR_CHUNK
    for chunk in range(ROWS // CHUNK):
        span = slice(chunk * CHUNK, chunk * CHUNK + CHUNK)
        block = jnp.concatenate(
            [
                jnp.where(diagonal, table[head : head + 1, span], 0.0)
                for head in range(HEADS_DEV)
            ],
            axis=0,
        )
        high = block.astype(BF16)
        low = (block - high.astype(F32)).astype(BF16)
        pair = jnp.dot(
            jnp.concatenate([high, low], axis=0), patches[span], preferred_element_type=F32
        )
        pair = pair[0:stacked] + pair[stacked : 2 * stacked]
        pick = iota((VAR_CHUNK, 128), 1) == iota((VAR_CHUNK, 128), 0) + chunk * VAR_CHUNK
        for head in range(HEADS_DEV):
            base = jnp.sum(
                jnp.where(pick, table[head : head + 1, ROWS:DEPTH], 0.0), axis=1, keepdims=True
            )
            scores[head, chunk * VAR_CHUNK : (chunk + 1) * VAR_CHUNK] = (
                pair[head * VAR_CHUNK : (head + 1) * VAR_CHUNK] + base
            )
    spread = (lax.div(iota((CHUNK, VAR_CHUNK), 0), PIX) == iota((CHUNK, VAR_CHUNK), 1)).astype(
        BF16
    )

    flags = jnp.broadcast_to(mask[...].astype(F32).reshape(1, VARS), (VARS, VARS))
    keep = jnp.sum(
        jnp.where(iota((VARS, VARS), 0) == iota((VARS, VARS), 1), flags, 0.0),
        axis=1,
        keepdims=True,
    )

    def weigh(head):
        raised = jnp.exp(scores[head]) * keep
        attention[head] = (raised / jnp.sum(raised, axis=0, keepdims=True)).astype(BF16)
        for chunk in range(ROWS // CHUNK):
            span = slice(chunk * CHUNK, chunk * CHUNK + CHUNK)
            wide = jnp.dot(
                spread,
                attention[head, chunk * VAR_CHUNK : (chunk + 1) * VAR_CHUNK],
                preferred_element_type=F32,
            )
            weighted[head, span] = wide.astype(BF16) * patches[span]
        weighted[head, ROWS : ROWS + VARS] = attention[head]
        weighted[head, ROWS + VARS :] = jnp.zeros((DEPTH - ROWS - VARS, TOK), BF16)

    for head in range(HEADS_DEV):
        weigh(head)

    o_gather.serve(2, 1)
    u_gather.line(3)
    u_gather.ring()
    o_gather.ring(0)
    o_gather.ring(1)
    o_gather.ring(2)
    o_gather.ring(3)
    project(0, 0)
    project(-1, 0)
    project(1, 0)
    u_gather.sibling(0)
    project(0, 1)
    u_gather.sibling(-1)
    project(-1, 1)
    u_gather.sibling(1)
    project(1, 1)
    u_gather.far()
    project(2, 0)
    u_gather.sibling(2)
    project(2, 1)

    def partial(target, dst):
        near = target * 8 + half * 4
        far = (3 - target) * 8 + (1 - half) * 4 + 2
        for quarter in range(4):
            own_rows = jnp.dot(
                heads[:, pl.ds(pl.multiple_of(half * 512, 512), 512)],
                o_all[near + quarter],
                preferred_element_type=F32,
            )
            other_rows = jnp.dot(
                heads[:, pl.ds(pl.multiple_of(512 - half * 512, 512), 512)],
                o_all[far + quarter - 4 * (quarter // 2)],
                preferred_element_type=F32,
            )
            dst[:, quarter * 128 : quarter * 128 + 128] = (own_rows + other_rows).astype(
                dst.dtype
            )

    low_rows, high_rows = pl.ds(0, 128), pl.ds(128, 128)
    to_right, to_left = (targets[1] * 2 + half, seat), (targets[2] * 2 + half, seat)

    def pass_on(src, dst, slot, target):
        remote(src, dst, p_send.at[0], p_recv.at[slot], target).start()

    def block(turn, dst):
        o_gather.far(turn)
        o_gather.sibling(turn)
        partial(targets[turn], dst)

    block(0, part_out.at[0])
    pass_on(part_out.at[0, low_rows], part_in.at[0, low_rows], 0, to_right)
    pass_on(part_out.at[0, high_rows], part_in.at[0, high_rows], 1, to_left)
    block(1, part_out.at[1])
    pass_on(part_out.at[1, high_rows], part_in.at[1, high_rows], 2, to_right)
    block(2, part_out.at[2])
    pass_on(part_out.at[2, low_rows], part_in.at[2, low_rows], 3, to_left)
    landed(part_in.at[0, low_rows], p_recv.at[0])
    part_out[1, 0:128] = (
        part_out[1, 0:128].astype(F32) + part_in[0, 0:128].astype(F32)
    ).astype(BF16)
    pass_on(part_out.at[1, low_rows], part_in.at[1, low_rows], 4, to_right)
    landed(part_in.at[0, high_rows], p_recv.at[1])
    part_out[2, 128:256] = (
        part_out[2, 128:256].astype(F32) + part_in[0, 128:256].astype(F32)
    ).astype(BF16)
    pass_on(part_out.at[2, high_rows], part_in.at[2, high_rows], 5, to_left)
    block(3, total)
    landed(part_in.at[1, high_rows], p_recv.at[2])
    landed(part_in.at[2, low_rows], p_recv.at[3])
    landed(part_in.at[1, low_rows], p_recv.at[4])
    landed(part_in.at[2, high_rows], p_recv.at[5])
    offset = bias[...].astype(F32).reshape(1, COLS)
    out[...] = (
        total[...] + part_in[1].astype(F32) + part_in[2].astype(F32) + offset
    ).astype(BF16)

    o_gather.finish()
    u_gather.finish()
    left(u_in_x, x_sem.at[0])

    @pl.when(first_core)
    def _():
        left(table_in, t_sem.at[0])
        table_copy.wait_send()
        table_share.wait_send()

    left(part_out, p_send.at[0])
    pl.when(swaps)(swap.wait_send)
    for which in range(2):
        pl.when(jnp.logical_not(here[which]))(fold[which].wait_send)


def local(
    patches, embed_weight, var_embed, key_query, var_mask, value_weight, out_weight, out_bias
):
    vmem = pl.BlockSpec(memory_space=pltpu.VMEM)
    hbm = pl.BlockSpec(memory_space=pl.ANY)
    sems = pltpu.SemaphoreType.DMA
    return pl.pallas_call(
        kernel,
        out_shape=jax.ShapeDtypeStruct((TOK, COLS), BF16),
        in_specs=[hbm] * 8,
        out_specs=vmem,
        scratch_shapes=[
            pltpu.VMEM((VARS,), jnp.int32),
            pltpu.VMEM((COLS,), BF16),
            pltpu.VMEM((ROWS, TOK), BF16),
            pltpu.VMEM((ROWS, COLS), BF16),
            pltpu.VMEM((128, COLS), BF16),
            pltpu.VMEM((COLS, 128), BF16),
            pltpu.VMEM((160, COLS), BF16),
            pltpu.VMEM((32, COLS, 128), BF16),
            pltpu.VMEM((64, 16, DEPTH), BF16),
            pltpu.VMEM((4, 8, DEPTH), F32),
            pltpu.VMEM((3, 8, DEPTH), F32),
            pltpu.VMEM((8, DEPTH), F32),
            pltpu.VMEM((8, DEPTH), F32),
            pltpu.VMEM((8, DEPTH), F32),
            pltpu.VMEM((8, 16, DEPTH), BF16),
            pltpu.VMEM((3, 2, 16, DEPTH), BF16),
            pltpu.VMEM((2, 16, DEPTH), BF16),
            pltpu.VMEM((2, 16, DEPTH), BF16),
            pltpu.VMEM((HEADS_DEV, VARS, TOK), F32),
            pltpu.VMEM((HEADS_DEV, VARS, TOK), BF16),
            pltpu.VMEM((HEADS_DEV, DEPTH, TOK), BF16),
            pltpu.VMEM((TOK, 1024), BF16),
            pltpu.VMEM((3, TOK, COLS), BF16),
            pltpu.VMEM((3, TOK, COLS), BF16),
            pltpu.VMEM((TOK, COLS), F32),
            sems((16,)),
            sems((2,)),
            sems((16,)),
            sems((4,)),
            sems((1,)),
            sems((32,)),
            sems((4,)),
            sems((1,)),
            sems((6,)),
            sems((2,)),
            sems((2,)),
            sems((2,)),
            sems((1,)),
            sems((6,)),
        ],
        compiler_params=pltpu.CompilerParams(
            has_side_effects=True, collective_id=0, vmem_limit_bytes=56 * 1024 * 1024
        ),
        cost_estimate=pl.CostEstimate(
            flops=2_000_000_000, bytes_accessed=4_000_000, transcendentals=200_000
        ),
        name="aggregate",
    )(
        patches.reshape(ROWS, TOK),
        embed_weight.reshape(ROWS, COLS),
        var_embed,
        key_query.T,
        value_weight.reshape(COLS, 128),
        out_weight,
        var_mask,
        out_bias,
    )


def solution(mesh):
    placed = (
        P(None, None, "seq"),
        P(None, None, "var"),
        P(None, "var"),
        P("var", None),
        P(),
        P("var", "seq", None),
        P("var", "seq"),
        P("var"),
    )
    return jax.shard_map(
        local, mesh=mesh, in_specs=placed, out_specs=P("seq", "var"), check_vma=False
    )
```

```python
import jax
import jax.numpy as jnp
from jax import lax
from jax.experimental import pallas as pl
from jax.experimental.pallas import tpu as pltpu
from jax.sharding import PartitionSpec as P

MESH = pl.DeviceIdType.MESH
F32 = jnp.float32
BF16 = jnp.bfloat16
VARS, PIX, TOK = 96, 16, 256
ROWS = VARS * PIX
DEPTH = ROWS + 128
CHUNK = 256
VAR_CHUNK = CHUNK // PIX
HEADS_DEV = 8
COLS = 512


def iota(shape, dim):
    return lax.broadcasted_iota(jnp.int32, shape, dim)


def kernel(
    patches_hbm,
    weight_hbm,
    embed_hbm,
    query_hbm,
    value_hbm,
    out_weight,
    mask_hbm,
    bias_hbm,
    out,
    mask,
    bias,
    patches,
    weight,
    embed_pad,
    value,
    left_side,
    o_all,
    u_all,
    table_out,
    table_in,
    table_mid,
    table_far,
    table,
    u_part,
    u_in_x,
    u_mid,
    u_in_z,
    scores,
    attention,
    weighted,
    heads,
    part_out,
    part_in,
    total,
    l_sem,
    o_send,
    o_recv,
    o_near,
    u_send,
    u_recv,
    u_near,
    o_swap,
    t_sem,
    x_sem,
    z_send,
    z_recv,
    p_send,
    p_recv,
):
    me = lax.axis_index("var")
    seat = lax.axis_index("seq")
    x, half = lax.div(me, 2), lax.rem(me, 2)
    zlo, y, core = lax.div(seat, 8), lax.rem(lax.div(seat, 2), 4), lax.rem(seat, 2)
    lane = lax.rem(seat, 8)
    z = half * 4 + zlo

    def turned(dz, dy, dc=0):
        return (
            lax.rem(z + dz + 8, 8),
            lax.rem(y + dy + 4, 4),
            lax.rem(core + dc, 2),
        )

    def device(z2, y2, c2):
        return (x * 2 + lax.div(z2, 4), lax.rem(z2, 4) * 8 + y2 * 2 + c2)

    loads = [
        pltpu.make_async_copy(value_hbm, value, l_sem.at[0]),
        pltpu.make_async_copy(query_hbm, left_side.at[pl.ds(128, 32)], l_sem.at[1]),
        pltpu.make_async_copy(embed_hbm, embed_pad.at[pl.ds(0, VARS)], l_sem.at[2]),
    ]
    weight_loads = []
    for part in range(6):
        span = pl.ds(part * 256, 256)
        weight_loads.append(
            pltpu.make_async_copy(weight_hbm.at[span], weight.at[span], l_sem.at[10 + part])
        )
    loads.append(pltpu.make_async_copy(patches_hbm, patches, l_sem.at[6]))
    loads.append(pltpu.make_async_copy(mask_hbm, mask, l_sem.at[8]))
    loads.append(pltpu.make_async_copy(bias_hbm, bias, l_sem.at[9]))

    for copy in loads[:3] + weight_loads + loads[3:]:
        copy.start()

    swaps = lax.div(y, 2) != half
    swap_to = (x * 2 + 1 - half, (3 - zlo) * 8 + (3 - y) * 2 + core)
    fold_seat = x * 8 + lane
    here = [
        jnp.logical_and(zlo * 2 + which == me, fold_seat == seat) for which in range(2)
    ]
    barrier = pltpu.get_barrier_semaphore()

    def greet(target):
        pl.semaphore_signal(barrier, inc=1, device_id=target, device_id_type=MESH)

    for dx in (1, 2, 3):
        greet((lax.rem(x + dx, 4) * 2 + half, seat))
    for dz in (4, 1, -1):
        greet(device(*turned(dz, 0)))
    pl.when(lax.rem(zlo, 3) == 0)(lambda: greet((me, jnp.where(zlo == 0, 2, 1) * 8 + lane)))
    pl.when(lax.rem(zlo, 3) > 0)(lambda: greet((me, lax.rem(zlo + 2, 4) * 8 + lane)))
    for dy in (1, -1):
        greet(device(*turned(0, dy)))
    greet(device(*turned(0, 0, 1)))
    for which in range(2):

        @pl.when(jnp.logical_not(here[which]))
        def _():
            greet((zlo * 2 + which, fold_seat))

    pl.when(lax.rem(zlo, 3) == 0)(lambda: greet((me, (3 - zlo) * 8 + lane)))
    pl.when(swaps)(lambda: greet(swap_to))

    stay = pltpu.make_async_copy(out_weight, o_all.at[seat], l_sem.at[7])

    @pl.when(jnp.logical_not(swaps))
    def _():
        stay.start()

    def remote(src, dst, send, recv, target):
        return pltpu.make_async_remote_copy(
            src_ref=src,
            dst_ref=dst,
            send_sem=send,
            recv_sem=recv,
            device_id=target,
            device_id_type=MESH,
        )

    def push(buf, piece, send, recv, target):
        remote(buf.at[piece], buf.at[piece], send, recv, device(*target)).start()

    def landed(ref, recv):
        remote(ref, ref, recv, recv, (me, seat)).wait_recv()

    def left(ref, send):
        remote(ref, ref, send, send, (me, seat)).wait_send()

    class FoldedGather:
        steps = (1, -1, 2, -2, 3, -3, 4)

        def index(self, z2, y2, c2):
            return (y2 * 2 + c2) * 8 + lax.rem(z2, 4) * 2 + lax.div(z2, 4)

        def push(self, spot, target):
            push(u_all, self.index(*spot), u_send.at[0], u_recv.at[spot[1] * 8 + spot[0]], target)

        def arrive(self, spot):
            landed(u_all.at[self.index(*spot)], u_recv.at[spot[1] * 8 + spot[0]])

        def near(self, spot):
            push(u_all, self.index(*spot), u_send.at[0], u_near.at[spot[1]], turned(0, 0, 1))

        def sides(self, spot):
            self.push(spot, turned(0, 1))
            self.push(spot, turned(0, -1))
            self.near(spot)

        def own(self):
            for sign in (1, -1):
                self.push(turned(0, 0), turned(sign, 0))
            self.sides(turned(0, 0))

        def line(self, distance):
            if distance < 3:
                for sign in (1, -1):
                    spot = turned(-sign * distance, 0)
                    self.arrive(spot)
                    self.push(spot, turned(sign, 0))
                    self.sides(spot)
                return
            for sign in (1, -1):
                self.arrive(turned(-3 * sign, 0))
            around = 1 - 2 * core
            self.push(turned(-3 * around, 0), turned(around, 0))
            for step in (3, -3, 4):
                if step == 4:
                    self.arrive(turned(4, 0))
                self.sides(turned(step, 0))

        def ring(self):
            for place, step in enumerate((0,) + self.steps):
                left, right = turned(-step, -1), turned(-step, 1)
                self.arrive(left)
                if place % 2 == 0:
                    self.push(left, turned(0, 1))
                self.near(left)
                self.arrive(right)
                if place % 2 == 1:
                    self.push(right, turned(0, -1))
                self.near(right)

        def far(self):
            for step in (0,) + self.steps:
                self.arrive(turned(-step, 2))
                self.near(turned(-step, 2))

        def sibling(self, dy):
            y2 = lax.rem(y + dy + 4, 4)
            landed(u_all.at[pl.ds((y2 * 2 + 1 - core) * 8, 8)], u_near.at[y2])

        def finish(self):
            left(u_all.at[pl.ds(0, 63)], u_send.at[0])

    targets = [lax.rem(x + dx, 4) for dx in (2, 1, 3, 0)]

    class OutGather:
        def __init__(self):
            middle = jnp.logical_and(zlo > 0, zlo < 3)
            twice, mirror = lax.rem(zlo + 2, 4), 3 - zlo
            self.lines = (
                zlo + 1 - 2 * lax.rem(zlo, 2),
                jnp.where(middle, mirror, twice),
                jnp.where(middle, twice, mirror),
            )

        def spot(self, turn, dy, dc=0):
            y2, target = lax.rem(y + dy + 4, 4), targets[turn]
            near = (lax.div(y2, 2) == half).astype(jnp.int32)
            line = near * target + (1 - near) * (3 - target)
            return half * 4 + line, y2, lax.rem(core + dc, 2)

        def index(self, z2, y2, c2):
            return lax.rem(z2, 4) * 8 + y2 * 2 + c2

        def push(self, spot, target, kind):
            recv = o_recv.at[lax.rem(spot[0], 4) * 4 + spot[1]]
            push(o_all, self.index(*spot), o_send.at[kind], recv, target)

        def arrive(self, spot):
            landed(o_all.at[self.index(*spot)], o_recv.at[lax.rem(spot[0], 4) * 4 + spot[1]])

        def near(self, spot):
            line = lax.rem(spot[0], 4)
            target = jnp.where(lax.div(spot[1], 2) == half, line, 3 - line)
            push(o_all, self.index(*spot), o_send.at[0], o_near.at[target], turned(0, 0, 1))

        def sides(self, spot):
            self.push(spot, turned(0, 1), 0)
            self.push(spot, turned(0, -1), 0)
            self.near(spot)

        def own(self):
            mine = turned(0, 0)
            for line in self.lines:
                self.push(mine, (half * 4 + line, y, core), 1)
            self.sides(mine)

        def serve(self, order, crossed):
            spot = (half * 4 + self.lines[order], y, core)

            @pl.when(swaps if crossed else jnp.logical_not(swaps))
            def _():
                self.arrive(spot)
                self.sides(spot)

        def ring(self, turn):
            prior, following = self.spot(turn, -1), self.spot(turn, 1)
            self.arrive(prior)
            if turn % 2 == 0:
                self.push(prior, turned(0, 1), 0)
            self.near(prior)
            self.arrive(following)
            if turn % 2 == 1:
                self.push(following, turned(0, -1), 0)
            self.near(following)

        def far(self, turn):
            spot = self.spot(turn, 2)
            self.arrive(spot)
            self.near(spot)

        def sibling(self, turn):
            landed(o_all.at[pl.ds(0, 4)], o_near.at[targets[turn]])

        def finish(self):
            left(o_all.at[pl.ds(0, 28)], o_send.at[0])
            left(o_all.at[pl.ds(0, 3)], o_send.at[1])

    o_gather = OutGather()
    u_gather = FoldedGather()
    swap_piece = (3 - zlo) * 8 + (3 - y) * 2 + core
    swap = remote(
        out_weight,
        o_all.at[swap_piece],
        o_swap.at[0],
        o_recv.at[(3 - zlo) * 4 + 3 - y],
        swap_to,
    )

    embed_pad[VARS:] = jnp.zeros((128 - VARS, COLS), BF16)
    for copy in loads[:3]:
        copy.wait()
    left_side[0:128] = value[...].astype(F32).T.astype(BF16)
    for part in (3, 0, 1, 2):
        wide = 512 if part < 3 else 128
        if part < 3:
            weight_loads[2 * part].wait()
            weight_loads[2 * part + 1].wait()
            rhs = weight[part * 512 : part * 512 + 512]
        else:
            rhs = embed_pad[...]
        both = lax.dot_general(
            left_side[...], rhs, (((1,), (1,)), ((), ())), preferred_element_type=F32
        )
        for group in range(8):
            u_part[group, :, part * 512 : part * 512 + wide] = both[
                group * 16 : group * 16 + 16
            ].astype(BF16)
        for group in range(4):
            table_out[group, :, part * 512 : part * 512 + wide] = both[
                128 + group * 8 : 136 + group * 8
            ]

    pl.semaphore_wait(
        barrier, 12 + (lax.rem(zlo, 3) == 0).astype(jnp.int32) - here[0].astype(jnp.int32) - here[1].astype(jnp.int32) + swaps.astype(jnp.int32)
    )

    for dx in (2, 1, 3):
        target = lax.rem(x + dx, 4)
        remote(
            u_part.at[pl.ds(target * 2, 2)],
            u_in_x.at[dx - 1],
            x_sem.at[0],
            x_sem.at[1],
            (target * 2 + half, seat),
        ).start()

    @pl.when(swaps)
    def _():
        swap.start()

    @pl.when(jnp.logical_not(swaps))
    def _():
        stay.wait()
        o_gather.own()

    landed(u_in_x, x_sem.at[1])
    for which in range(2):
        u_mid[which] = (
            u_part[x * 2 + which].astype(F32)
            + u_in_x[0, which].astype(F32)
            + u_in_x[1, which].astype(F32)
            + u_in_x[2, which].astype(F32)
        ).astype(BF16)
    fold = []
    for which in range(2):
        copy = remote(
            u_mid.at[which],
            u_in_z.at[half],
            z_send.at[which],
            z_recv.at[half],
            (zlo * 2 + which, fold_seat),
        )
        fold.append(copy)
        pl.when(jnp.logical_not(here[which]))(copy.start)

        @pl.when(here[which])
        def _():
            u_in_z[half] = u_mid[which]

    first_core = core == 0
    table_copy = remote(
        table_mid, table_far, t_sem.at[2], t_sem.at[3], (x * 2 + 1 - half, seat)
    )
    table_share = remote(
        table, table, t_sem.at[4], t_sem.at[5], device(*turned(0, 0, 1))
    )

    def table_start():
        @pl.when(first_core)
        def _():
            for dx in (2, 1, 3):
                target = lax.rem(x + dx, 4)
                remote(
                    table_out.at[target],
                    table_in.at[dx - 1],
                    t_sem.at[0],
                    t_sem.at[1],
                    (target * 2 + half, seat),
                ).start()

    def table_pass():
        @pl.when(first_core)
        def _():
            landed(table_in, t_sem.at[1])
            table_mid[...] = table_out[x] + table_in[0] + table_in[1] + table_in[2]
            table_copy.start()

    def table_end():
        @pl.when(first_core)
        def _():
            table_copy.wait_recv()
            table[...] = table_mid[...] + table_far[...]
            table_share.start()

        pl.when(jnp.logical_not(first_core))(table_share.wait_recv)

    def reduce_z():
        for source in range(2):

            @pl.when(jnp.logical_not(here[source]))
            def _():
                landed(u_in_z.at[source], z_recv.at[source])

        u_all[lane * 8 + zlo * 2 + half] = (
            u_in_z[0].astype(F32) + u_in_z[1].astype(F32)
        ).astype(BF16)

    def project(dy, dc):
        head = lax.rem(y + dy + 4, 4) * 2 + lax.rem(core + dc, 2)
        columns = jnp.dot(
            u_all[pl.ds(head * 8, 8)].reshape(128, DEPTH),
            weighted[head],
            preferred_element_type=F32,
        )
        heads[:, pl.ds(pl.multiple_of(head * 128, 128), 128)] = columns.T.astype(BF16)

    table_start()
    o_gather.serve(0, 0)
    reduce_z()
    u_gather.own()

    @pl.when(swaps)
    def _():
        o_gather.arrive(turned(0, 0))
        o_gather.own()

    o_gather.serve(1, 0)
    o_gather.serve(2, 0)
    u_gather.line(1)
    table_pass()
    o_gather.serve(0, 1)
    o_gather.serve(1, 1)
    u_gather.line(2)
    for copy in loads[3:]:
        copy.wait()
    table_end()
    diagonal = lax.div(iota((VAR_CHUNK, CHUNK), 1), PIX) == iota((VAR_CHUNK, CHUNK), 0)
    stacked = HEADS_DEV * VAR_CHUNK
    for chunk in range(ROWS // CHUNK):
        span = slice(chunk * CHUNK, chunk * CHUNK + CHUNK)
        block = jnp.concatenate(
            [
                jnp.where(diagonal, table[head : head + 1, span], 0.0)
                for head in range(HEADS_DEV)
            ],
            axis=0,
        )
        high = block.astype(BF16)
        low = (block - high.astype(F32)).astype(BF16)
        pair = jnp.dot(
            jnp.concatenate([high, low], axis=0), patches[span], preferred_element_type=F32
        )
        pair = pair[0:stacked] + pair[stacked : 2 * stacked]
        pick = iota((VAR_CHUNK, 128), 1) == iota((VAR_CHUNK, 128), 0) + chunk * VAR_CHUNK
        for head in range(HEADS_DEV):
            base = jnp.sum(
                jnp.where(pick, table[head : head + 1, ROWS:DEPTH], 0.0), axis=1, keepdims=True
            )
            scores[head, chunk * VAR_CHUNK : (chunk + 1) * VAR_CHUNK] = (
                pair[head * VAR_CHUNK : (head + 1) * VAR_CHUNK] + base
            )
    spread = (lax.div(iota((CHUNK, VAR_CHUNK), 0), PIX) == iota((CHUNK, VAR_CHUNK), 1)).astype(
        BF16
    )

    flags = jnp.broadcast_to(mask[...].astype(F32).reshape(1, VARS), (VARS, VARS))
    keep = jnp.sum(
        jnp.where(iota((VARS, VARS), 0) == iota((VARS, VARS), 1), flags, 0.0),
        axis=1,
        keepdims=True,
    )

    def weigh(head):
        raised = jnp.exp(scores[head]) * keep
        attention[head] = (raised / jnp.sum(raised, axis=0, keepdims=True)).astype(BF16)
        for chunk in range(ROWS // CHUNK):
            span = slice(chunk * CHUNK, chunk * CHUNK + CHUNK)
            wide = jnp.dot(
                spread,
                attention[head, chunk * VAR_CHUNK : (chunk + 1) * VAR_CHUNK],
                preferred_element_type=F32,
            )
            weighted[head, span] = wide.astype(BF16) * patches[span]
        weighted[head, ROWS : ROWS + VARS] = attention[head]
        weighted[head, ROWS + VARS :] = jnp.zeros((DEPTH - ROWS - VARS, TOK), BF16)

    for head in range(HEADS_DEV):
        weigh(head)

    o_gather.serve(2, 1)
    u_gather.line(3)
    project(0, 0)
    u_gather.ring()
    o_gather.ring(0)
    o_gather.ring(1)
    o_gather.ring(2)
    o_gather.ring(3)
    project(-1, 0)
    project(1, 0)
    u_gather.sibling(0)
    project(0, 1)
    u_gather.sibling(-1)
    project(-1, 1)
    u_gather.sibling(1)
    project(1, 1)
    u_gather.far()
    project(2, 0)
    u_gather.sibling(2)
    project(2, 1)

    def partial(target, dst):
        near = target * 8 + half * 4
        far = (3 - target) * 8 + (1 - half) * 4 + 2
        for quarter in range(4):
            own_rows = jnp.dot(
                heads[:, pl.ds(pl.multiple_of(half * 512, 512), 512)],
                o_all[near + quarter],
                preferred_element_type=F32,
            )
            other_rows = jnp.dot(
                heads[:, pl.ds(pl.multiple_of(512 - half * 512, 512), 512)],
                o_all[far + quarter - 4 * (quarter // 2)],
                preferred_element_type=F32,
            )
            dst[:, quarter * 128 : quarter * 128 + 128] = (own_rows + other_rows).astype(
                dst.dtype
            )

    low_rows, high_rows = pl.ds(0, 128), pl.ds(128, 128)
    to_right, to_left = (targets[1] * 2 + half, seat), (targets[2] * 2 + half, seat)

    def pass_on(src, dst, slot, target):
        remote(src, dst, p_send.at[0], p_recv.at[slot], target).start()

    def block(turn, dst):
        o_gather.far(turn)
        o_gather.sibling(turn)
        partial(targets[turn], dst)

    block(0, part_out.at[0])
    pass_on(part_out.at[0, low_rows], part_in.at[0, low_rows], 0, to_right)
    pass_on(part_out.at[0, high_rows], part_in.at[0, high_rows], 1, to_left)
    block(1, part_out.at[1])
    pass_on(part_out.at[1, high_rows], part_in.at[1, high_rows], 2, to_right)
    block(2, part_out.at[2])
    pass_on(part_out.at[2, low_rows], part_in.at[2, low_rows], 3, to_left)
    landed(part_in.at[0, low_rows], p_recv.at[0])
    part_out[1, 0:128] = (
        part_out[1, 0:128].astype(F32) + part_in[0, 0:128].astype(F32)
    ).astype(BF16)
    pass_on(part_out.at[1, low_rows], part_in.at[1, low_rows], 4, to_right)
    landed(part_in.at[0, high_rows], p_recv.at[1])
    part_out[2, 128:256] = (
        part_out[2, 128:256].astype(F32) + part_in[0, 128:256].astype(F32)
    ).astype(BF16)
    pass_on(part_out.at[2, high_rows], part_in.at[2, high_rows], 5, to_left)
    block(3, total)
    landed(part_in.at[1, high_rows], p_recv.at[2])
    landed(part_in.at[2, low_rows], p_recv.at[3])
    landed(part_in.at[1, low_rows], p_recv.at[4])
    landed(part_in.at[2, high_rows], p_recv.at[5])
    offset = bias[...].astype(F32).reshape(1, COLS)
    out[...] = (
        total[...] + part_in[1].astype(F32) + part_in[2].astype(F32) + offset
    ).astype(BF16)

    o_gather.finish()
    u_gather.finish()
    left(u_in_x, x_sem.at[0])

    @pl.when(first_core)
    def _():
        left(table_in, t_sem.at[0])
        table_copy.wait_send()
        table_share.wait_send()

    left(part_out, p_send.at[0])
    pl.when(swaps)(swap.wait_send)
    for which in range(2):
        pl.when(jnp.logical_not(here[which]))(fold[which].wait_send)


def local(
    patches, embed_weight, var_embed, key_query, var_mask, value_weight, out_weight, out_bias
):
    vmem = pl.BlockSpec(memory_space=pltpu.VMEM)
    hbm = pl.BlockSpec(memory_space=pl.ANY)
    sems = pltpu.SemaphoreType.DMA
    return pl.pallas_call(
        kernel,
        out_shape=jax.ShapeDtypeStruct((TOK, COLS), BF16),
        in_specs=[hbm] * 8,
        out_specs=vmem,
        scratch_shapes=[
            pltpu.VMEM((VARS,), jnp.int32),
            pltpu.VMEM((COLS,), BF16),
            pltpu.VMEM((ROWS, TOK), BF16),
            pltpu.VMEM((ROWS, COLS), BF16),
            pltpu.VMEM((128, COLS), BF16),
            pltpu.VMEM((COLS, 128), BF16),
            pltpu.VMEM((160, COLS), BF16),
            pltpu.VMEM((32, COLS, 128), BF16),
            pltpu.VMEM((64, 16, DEPTH), BF16),
            pltpu.VMEM((4, 8, DEPTH), F32),
            pltpu.VMEM((3, 8, DEPTH), F32),
            pltpu.VMEM((8, DEPTH), F32),
            pltpu.VMEM((8, DEPTH), F32),
            pltpu.VMEM((8, DEPTH), F32),
            pltpu.VMEM((8, 16, DEPTH), BF16),
            pltpu.VMEM((3, 2, 16, DEPTH), BF16),
            pltpu.VMEM((2, 16, DEPTH), BF16),
            pltpu.VMEM((2, 16, DEPTH), BF16),
            pltpu.VMEM((HEADS_DEV, VARS, TOK), F32),
            pltpu.VMEM((HEADS_DEV, VARS, TOK), BF16),
            pltpu.VMEM((HEADS_DEV, DEPTH, TOK), BF16),
            pltpu.VMEM((TOK, 1024), BF16),
            pltpu.VMEM((3, TOK, COLS), BF16),
            pltpu.VMEM((3, TOK, COLS), BF16),
            pltpu.VMEM((TOK, COLS), F32),
            sems((16,)),
            sems((2,)),
            sems((16,)),
            sems((4,)),
            sems((1,)),
            sems((32,)),
            sems((4,)),
            sems((1,)),
            sems((6,)),
            sems((2,)),
            sems((2,)),
            sems((2,)),
            sems((1,)),
            sems((6,)),
        ],
        compiler_params=pltpu.CompilerParams(
            has_side_effects=True, collective_id=0, vmem_limit_bytes=56 * 1024 * 1024
        ),
        cost_estimate=pl.CostEstimate(
            flops=2_000_000_000, bytes_accessed=4_000_000, transcendentals=200_000
        ),
        name="aggregate",
    )(
        patches.reshape(ROWS, TOK),
        embed_weight.reshape(ROWS, COLS),
        var_embed,
        key_query.T,
        value_weight.reshape(COLS, 128),
        out_weight,
        var_mask,
        out_bias,
    )


def solution(mesh):
    placed = (
        P(None, None, "seq"),
        P(None, None, "var"),
        P(None, "var"),
        P("var", None),
        P(),
        P("var", "seq", None),
        P("var", "seq"),
        P("var"),
    )
    return jax.shard_map(
        local, mesh=mesh, in_specs=placed, out_specs=P("seq", "var"), check_vma=False
    )
```
